128 devices in a mesh: expert: 32 (over y, z, core), fsdp: 4 (over x).
Axes of the slice: x: 4, y: 4, z: 4, core: 2. Of those that a mesh axis runs over, the one named last changes fastest.
Arguments:
- tokens: bfloat16 [25216, 768], P(('expert', 'fsdp')), may hold values from -6 to 6
- qkv_weight: bfloat16 [2, 3, 768, 768], P(None, None, 'fsdp'), may hold values from -0.21875 to 0.21875
- out_weight: bfloat16 [2, 768, 768], P(None, 'fsdp'), may hold values from -1.75 to 1.75
- norm_gain: bfloat16 [2, 2, 768], P(None, None, 'fsdp'), may hold values from 0.5 to 1.5
- mixer_bias: bfloat16 [2, 5, 768], P(None, None, 'fsdp'), may hold values from -1.25 to 1.25
- router_weight: bfloat16 [2, 768, 32], P(None, 'fsdp'), may hold values from -0.21875 to 0.21875
- router_bias: bfloat16 [2, 32], P(None, 'fsdp'), may hold values from -0.625 to 0.625
- expert_in: bfloat16 [2, 32, 768, 3072], P(None, 'expert', None, 'fsdp'), may hold values from -0.21875 to 0.21875
- expert_in_bias: bfloat16 [2, 32, 3072], P(None, 'expert', 'fsdp'), may hold values from -0.625 to 0.625
- expert_out: bfloat16 [2, 32, 3072, 768], P(None, 'expert', 'fsdp'), may hold values from -1.75 to 1.75
- expert_out_bias: bfloat16 [2, 32, 768], P(None, 'expert'), may hold values from -6 to 6
- routes: int32 [2, 25216, 2], P(None, ('expert', 'fsdp')), may hold values from 0 to 31, all different within a row; in each aligned block of 197 rows (0 to 196, 197 to 393, ..., all dimensions but the last counted through in order) at most 19 rows name the same one
- cotangent: bfloat16 [25216, 768], P(('expert', 'fsdp')), may hold values from -6 to 6
Outputs:
- activations: bfloat16 [25216, 768], P(('expert', 'fsdp'))
- tokens_grad: float32 [25216, 768], P(('expert', 'fsdp'))
- qkv_weight_grad: float32 [2, 3, 768, 768], P(None, None, 'fsdp')
- out_weight_grad: float32 [2, 768, 768], P(None, 'fsdp')
- norm_gain_grad: float32 [2, 2, 768], P(None, None, 'fsdp')
- mixer_bias_grad: float32 [2, 5, 768], P(None, None, 'fsdp')
- router_weight_grad: float32 [2, 768, 32], P(None, 'fsdp')
- router_bias_grad: float32 [2, 32], P(None, 'fsdp')
- expert_in_grad: float32 [2, 32, 768, 3072], P(None, 'expert', None, 'fsdp')
- expert_in_bias_grad: float32 [2, 32, 3072], P(None, 'expert', 'fsdp')
- expert_out_grad: float32 [2, 32, 3072, 768], P(None, 'expert', 'fsdp')
- expert_out_bias_grad: float32 [2, 32, 768], P(None, 'expert')
The draws below stay inside these ranges and needn't reach their ends.
Inputs may be any that keep to these rules, and one draw needn't show every extreme that they name: `routes`: the two experts of a token differ. Among the 197 tokens of one block in one layer at most 19 name one expert, and some block and expert reach 19 in every draw.
All inputs are finite; a program needn't handle non-finite values.
Results may differ from the reference program's by a relative error of at most 0.033.
Values may be sent and summed in bfloat16 or wider, within the bound.
No kernel may reach another device: no remote copies, remote signals or barrier semaphores. Data moves between devices by JAX's collectives and lax.ppermute only.
A program may use at most 256 MiB of HBM per device.

```python
import math
import jax
import jax.numpy as jnp
import numpy as np
from jax import lax

D = 768
HEADS = 12
FF = 3072
HEAD_DIM = 64
IMG_LEN = 197
LAYERS = 2
TOK_DEV = 197
TOKENS = 25216
EXPERTS = 32
CAP = 19
N_EXPERT = 32
N_FSDP = 4


def shard_levels(key, shape, split, low, largest):
    def one(axis_at, parts):
        draws = jax.random.uniform(jax.random.fold_in(jax.random.fold_in(key, 6), axis_at), (parts,), jnp.float32, low / len(split), largest / len(split))
        return jnp.repeat(jnp.exp(draws), shape[axis_at] // parts).reshape((-1,) + (1,) * (len(shape) - axis_at - 1))

    level = one(*split[0])
    for cut in split[1:]:
        level = level * one(*cut)
    return level


def shared_out(key, own, number, rows, count, top, limit, lean):
    ranking = jax.random.permutation(key, count)
    heavy_load, ordinary = shares(count, rows * top, limit, lean, True), shares(count, rows * top, limit, lean, False)
    places = jnp.arange(count)

    def named(sizes, rotation):
        used = int((sizes > 0).sum())
        fixed = max(1, used // 4)
        moved = fixed + (places - fixed + rotation * (used - fixed)) % max(1, count - fixed)
        return jnp.zeros((count,), jnp.int32).at[ranking[jnp.where(places < fixed, places, moved)]].set(jnp.asarray(sizes, jnp.int32))

    sizes = jnp.where(number % 4 == 0, named(heavy_load, number // 4), named(ordinary, number - number // 4 - 1))
    mixed = jax.random.permutation(jax.random.fold_in(own, 3), count)
    donor, receiver = mixed[0:count // 2 * 2:2], mixed[1:count // 2 * 2:2]
    margin = jnp.minimum(sizes[donor] - 1, limit - sizes[receiver]) // 2
    margin = jnp.where((donor == ranking[0]) | (receiver == ranking[0]) | (sizes[receiver] == 0), 0, jnp.maximum(margin, 0))
    moved = jax.random.randint(jax.random.fold_in(own, 4), (count // 2,), 0, 1 << 20) % (margin + 1)
    sizes = sizes.at[donor].add(-moved).at[receiver].add(moved)
    members = jnp.searchsorted(jnp.cumsum(sizes), jnp.arange(rows * top), side="right").astype(jnp.int32)
    grid = members.reshape(top, rows).T
    grid = grid[jax.random.permutation(jax.random.fold_in(own, 1), rows)]
    rotation = jax.random.randint(jax.random.fold_in(own, 2), (rows, 1), 0, top)
    return jnp.take_along_axis(grid, (jnp.arange(top)[None, :] + rotation) % top, axis=1)


def shares(count, total, bound, slope, full):
    weights = [(1 << 20) // math.isqrt(grade ** slope) + 1 for grade in range(1, count + 1)]
    largest = bound if full else min(bound, max(-(-total // count), total * weights[0] // sum(weights)))
    least = 1 if total - largest >= count - 1 else 0
    counts, rest = [largest] + [least] * (count - 1), total - largest - least * (count - 1)
    while rest > 0:
        movable = [i for i in range(1, count) if counts[i] < largest] or [i for i in range(1, count) if counts[i] < bound]
        mass, left = sum([weights[i] for i in movable]), rest
        for i in movable:
            more = min(bound - counts[i], max(1, left * weights[i] // mass), rest)
            counts[i] = counts[i] + more
            rest = rest - more
    return np.array(counts)


def bell_draw(rng, extent, scale, bound, cuts=(), kind=jnp.bfloat16):
    level = shard_levels(rng, extent, cuts, -0.22, 0.18) if cuts else 1.0
    drawn = jax.random.normal(rng, extent, jnp.float32) * scale * level
    return jnp.minimum(jnp.maximum(drawn, -bound), bound).astype(kind)


def setup_inputs(seed: int = 0) -> dict:
    key_list = jax.random.split(jax.random.key(seed), 14)
    tokens = bell_draw(key_list[0], (TOKENS, D), 1.0, 6.0, ((0, 128),))
    qkv_weight = bell_draw(key_list[1], (LAYERS, 3, D, D), D ** -0.5, 0.21875, ((2, 4),))
    out_weight = bell_draw(key_list[2], (LAYERS, D, D), (D // 64) ** -0.5, 1.75, ((1, 4),))
    norm_gain = jnp.clip(1.0 + 0.1 * jax.random.normal(key_list[3], (LAYERS, 2, D), jnp.float32), 0.5, 1.5).astype(jnp.bfloat16)
    mixer_bias = bell_draw(key_list[4], (LAYERS, 5, D), 0.2, 1.25, ((2, 4),))
    router_weight = bell_draw(key_list[5], (LAYERS, D, EXPERTS), D ** -0.5, 0.21875, ((1, 4),))
    router_bias = bell_draw(key_list[6], (LAYERS, EXPERTS), 0.1, 0.625, ((1, 4),))
    expert_in = bell_draw(key_list[7], (LAYERS, EXPERTS, D, FF), D ** -0.5, 0.21875, ((1, 32), (3, 4)))
    expert_in_bias = bell_draw(key_list[8], (LAYERS, EXPERTS, FF), 0.1, 0.625, ((1, 32), (2, 4)))
    expert_out = bell_draw(key_list[9], (LAYERS, EXPERTS, FF, D), (max(1, FF // 256)) ** -0.5, 1.75, ((1, 32), (2, 4)))
    expert_out_bias = bell_draw(key_list[10], (LAYERS, EXPERTS, D), 1.0, 6.0, ((1, 32),))
    routes_keys = jax.random.split(jax.random.fold_in(key_list[11], 1), LAYERS * TOKENS // TOK_DEV)
    routes_turns = jax.random.permutation(jax.random.fold_in(key_list[11], 3), LAYERS * TOKENS // TOK_DEV)
    routes = jax.vmap(lambda own, number: shared_out(jax.random.fold_in(key_list[11], 2), own, number, TOK_DEV, EXPERTS, 2, CAP, 1))(routes_keys, routes_turns).reshape((LAYERS, TOKENS, 2))
    cotangent = bell_draw(key_list[12], (TOKENS, D), 1.0, 6.0, ((0, 128),))
    return dict(tokens=tokens, qkv_weight=qkv_weight, out_weight=out_weight, norm_gain=norm_gain, mixer_bias=mixer_bias, router_weight=router_weight, router_bias=router_bias, expert_in=expert_in, expert_in_bias=expert_in_bias, expert_out=expert_out, expert_out_bias=expert_out_bias, routes=routes, cotangent=cotangent)


@jax.custom_vjp
def low(v):
    return lax.optimization_barrier(v.astype(jnp.bfloat16)).astype(jnp.float32)

@jax.custom_vjp
def low_back(v):
    return v

def low_keep(v):
    return (low(v), None)

def low_pass(kept, grad):
    return (grad,)

def back_keep(v):
    return (v, None)

def back_low(kept, grad):
    return (low(grad),)
low.defvjp(low_keep, low_pass)
low_back.defvjp(back_keep, back_low)
epsilon = 1e-06
group_images = 16
highest = lax.Precision.HIGHEST

def rounded_both(value):
    return low(low_back(value))

def product(left, right):
    return jnp.dot(left, right, precision=highest)

def normalize(values, gain, shift):
    centred = values - lax.optimization_barrier(jnp.mean(values, axis=-1, keepdims=True))
    spread = lax.optimization_barrier(jnp.mean(centred * centred, axis=-1, keepdims=True))
    return centred * lax.rsqrt(spread + epsilon) * gain + shift

def attend(pieces):
    query, keyset, values = pieces
    scores = jnp.einsum('bqhd,bkhd->bhqk', query, keyset, precision=highest) * HEAD_DIM ** (-0.5)
    scores = low_back(scores)
    weights = jax.nn.softmax(scores, axis=-1)
    return jnp.einsum('bhqk,bkhd->bqhd', low(weights), values, precision=highest)

def expert(pieces):
    inputs, weight_in, bias_in, weight_out, bias_out = pieces
    hidden = low_back(product(inputs, weight_in) + bias_in)
    active = low(jax.nn.gelu(hidden, approximate=False))
    return product(active, weight_out) + bias_out

def slot_table(routes_layer):
    devices = N_EXPERT * N_FSDP
    blocks = routes_layer.reshape(devices, TOK_DEV * 2).astype(jnp.int32)
    onehot = (blocks[:, :, None] == jnp.arange(EXPERTS, dtype=jnp.int32)[None, None, :]).astype(jnp.int32)
    earlier = jnp.cumsum(onehot, axis=1) - onehot
    position = lax.optimization_barrier(jnp.sum(earlier * onehot, axis=2))
    device_ids = jnp.arange(devices, dtype=jnp.int32)[:, None]
    return ((device_ids * EXPERTS + blocks) * CAP + position).reshape(-1).astype(jnp.int32)

def layer(hidden_state, qkv_w, out_w, gain_rows, bias_rows, router_w, router_b, weight_in, bias_in, weight_out, bias_out, routes_layer, slots):
    token_count = hidden_state.shape[0]
    devices = N_EXPERT * N_FSDP
    normed = low(normalize(hidden_state, gain_rows[0], bias_rows[0]))
    query = rounded_both(product(normed, qkv_w[0]) + bias_rows[1])
    keyset = rounded_both(product(normed, qkv_w[1]))
    values = rounded_both(product(normed, qkv_w[2]) + bias_rows[2])
    image_shape = (token_count // (group_images * IMG_LEN), group_images, IMG_LEN, HEADS, HEAD_DIM)
    mixed = lax.map(jax.checkpoint(attend), (query.reshape(image_shape), keyset.reshape(image_shape), values.reshape(image_shape)))
    mixed = rounded_both(mixed.reshape(token_count, D))
    hidden_state = hidden_state + low_back(product(mixed, out_w)) + bias_rows[3]
    normed = low(normalize(hidden_state, gain_rows[1], bias_rows[4]))
    logits = low_back(product(normed, router_w) + router_b)
    router_probs = jax.nn.softmax(logits, axis=-1)
    gates = jnp.take_along_axis(router_probs, routes_layer, axis=1)
    buffer = jnp.zeros((devices * EXPERTS * CAP, D), jnp.float32).at[slots].set(jnp.repeat(normed, 2, axis=0))
    buffer = low_back(buffer)
    per_expert = buffer.reshape(devices, EXPERTS, CAP, D).transpose(1, 0, 2, 3).reshape(EXPERTS, devices * CAP, D)
    results = lax.map(jax.checkpoint(expert), (per_expert, weight_in, bias_in, weight_out, bias_out))
    results = rounded_both(results)
    returned = results.reshape(EXPERTS, devices, CAP, D).transpose(1, 0, 2, 3).reshape(devices * EXPERTS * CAP, D)
    picked = returned[slots].reshape(token_count, 2, D)
    return hidden_state + lax.optimization_barrier(jnp.sum(gates[:, :, None] * picked, axis=1))

def reference(tokens, qkv_weight, out_weight, norm_gain, mixer_bias, router_weight, router_bias, expert_in, expert_in_bias, expert_out, expert_out_bias, routes, cotangent):
    slot_tables = [slot_table(routes[layer_index]) for layer_index in range(LAYERS)]

    def forward(inputs, qkv_all, out_all, gain_all, bias_all, router_all, router_bias_all, in_all, in_bias_all, out_expert_all, out_bias_all):
        hidden_state = inputs
        for layer_index in range(LAYERS):
            hidden_state = layer(hidden_state, qkv_all[layer_index], out_all[layer_index], gain_all[layer_index], bias_all[layer_index], router_all[layer_index], router_bias_all[layer_index], in_all[layer_index], in_bias_all[layer_index], out_expert_all[layer_index], out_bias_all[layer_index], routes[layer_index], slot_tables[layer_index])
        return hidden_state
    floats = tuple((array.astype(jnp.float32) for array in (tokens, qkv_weight, out_weight, norm_gain, mixer_bias, router_weight, router_bias, expert_in, expert_in_bias, expert_out, expert_out_bias)))
    result, pullback = jax.vjp(forward, *floats)
    gradients = pullback(cotangent.astype(jnp.float32))
    return (result.astype(jnp.bfloat16), gradients[0], gradients[1], gradients[2], gradients[3], gradients[4], gradients[5], gradients[6], gradients[7], gradients[8], gradients[9], gradients[10])
```

```python
import functools

import jax
import jax.numpy as jnp
from jax import lax
from jax.experimental import pallas as pl
from jax.experimental.pallas import tpu as pltpu
from jax.sharding import PartitionSpec as P

HEADS = 12
LAYERS = 2
EPSILON = 1e-06
BF16 = jnp.bfloat16
F32 = jnp.float32
VMEM_LIMIT = 56 * 1024 * 1024


def dot(left, right, left_dim=1, right_dim=0):
    return lax.dot_general(
        left, right, (((left_dim,), (right_dim,)), ((), ())), preferred_element_type=F32
    )


def shaped(shape, kind):
    return jax.ShapeDtypeStruct(shape, kind)


def standardize(values):
    centred = values - jnp.mean(values, axis=-1, keepdims=True)
    inverse = lax.rsqrt(jnp.mean(centred * centred, axis=-1, keepdims=True) + EPSILON)
    return centred * inverse, inverse


def norm_backward(grad_out, scaled, inverse, gain):
    grad_scaled = grad_out * gain
    mean_grad = jnp.mean(grad_scaled, axis=-1, keepdims=True)
    mean_cross = jnp.mean(grad_scaled * scaled, axis=-1, keepdims=True)
    grad_input = inverse * (grad_scaled - mean_grad - scaled * mean_cross)
    return (
        grad_input,
        jnp.sum(grad_out * scaled, axis=0, keepdims=True),
        jnp.sum(grad_out, axis=0, keepdims=True),
    )


def gelu_both(pre):
    size = jnp.abs(pre) * (0.5**0.5)
    t = 1.0 / (1.0 + 0.3275911 * size)
    poly = t * (
        0.254829592
        + t * (-0.284496736 + t * (1.421413741 + t * (-1.453152027 + t * 1.061405429)))
    )
    bell = jnp.exp(-(size * size))
    tail = (0.5 * poly) * bell
    cdf = jnp.where(pre >= 0.0, 1.0 - tail, tail)
    return pre * cdf, cdf + pre * bell * 0.3989422804014327


def slot_targets(routes_layer, experts, stride):
    flat = routes_layer.reshape(-1)
    count = flat.shape[0]
    onehot = (flat[:, None] == jnp.arange(experts, dtype=jnp.int32)[None, :]).astype(BF16)
    below = (jnp.arange(count)[None, :] < jnp.arange(count)[:, None]).astype(BF16)
    earlier = dot(below, onehot)
    position = jnp.sum(earlier * onehot.astype(F32), axis=1).astype(jnp.int32)
    return (flat * stride + position).reshape(-1, 2)


def slot_rows(targets_row, rows, which):
    tokens = targets_row.shape[1]
    slots = lax.broadcasted_iota(jnp.int32, (rows, tokens), 0)
    return (slots == targets_row[which : which + 1, :]).astype(F32).astype(BF16)


def slot_columns(targets, rows, which):
    tokens = targets.shape[0]
    slots = lax.broadcasted_iota(jnp.int32, (tokens, rows), 1)
    return (slots == targets[:, which : which + 1]).astype(F32).astype(BF16)


def expert_hot(routes, experts, which):
    places = lax.broadcasted_iota(jnp.int32, (routes.shape[0], experts), 1)
    return (places == routes[:, which : which + 1]).astype(F32)


def pair_lanes(tokens, head):
    lanes = lax.broadcasted_iota(jnp.int32, (tokens, 128), 1)
    return (lanes // 64) == head % 2


def place_weights(here_ref, own_ref, mine, theirs, full_ref):
    _, part, _ = own_ref.shape
    parts = full_ref.shape[1] // part
    me, core = here_ref[0], here_ref[1]

    def spot(ahead):
        return pl.ds(pl.multiple_of(lax.rem(me + ahead, parts) * part, part), part)

    for kind in range(4):
        full_ref[kind, spot(0), :] = own_ref[kind]
    for ahead, (mine_ref, theirs_ref) in enumerate(zip(mine, theirs), start=1):
        for half in range(2):
            full_ref[2 * core + half, spot(ahead), :] = mine_ref[half]
            full_ref[2 * (1 - core) + half, spot(ahead), :] = theirs_ref[half]


def mixer_forward_body(first, count, scale, experts, *refs):
    here_ref, own_ref = refs[:2]
    full_ref = refs[-1]
    place_weights(here_ref, own_ref, refs[2:5], refs[5:8], full_ref)
    refs = refs[8:-1]
    if first:
        (x_ref, lane_ref, router_ref, rbias_ref, routes_ref, row_ref) = refs[:6]
        outs = refs[6:]
        x = x_ref[...]
    else:
        (
            middle_ref,
            back_ref,
            gates_prev_ref,
            targets_prev_ref,
            cot_ref,
            lane_ref,
            router_ref,
            rbias_ref,
            routes_ref,
            row_ref,
        ) = refs[:10]
        outs = refs[10:]
        x = middle_ref[...]
        back = back_ref[...]
        for j in range(2):
            picked = dot(slot_columns(targets_prev_ref[...], back.shape[0], j), back)
            x = x + gates_prev_ref[:, j : j + 1] * picked
    middle_out, send_out, q_out, k_out, v_out, m_out, lse_out, probs_out, gates_out = outs[:9]
    if not first:
        outs[9][...] = x
    tokens, width = x.shape
    lane = lane_ref[...]
    scaled, _ = standardize(x)
    normed = (scaled * lane[0:1] + lane[2:3]).astype(BF16)
    q_out[...] = (dot(normed, full_ref[0]) + lane[3:4]).astype(BF16)
    k_out[...] = dot(normed, full_ref[1]).astype(BF16)
    v_out[...] = (dot(normed, full_ref[2]) + lane[4:5]).astype(BF16)
    valid = lax.broadcasted_iota(jnp.int32, (tokens, tokens), 1) < count
    log_totals = jnp.zeros((tokens, 128), F32)
    head_lanes = lax.broadcasted_iota(jnp.int32, (tokens, 128), 1)
    for pair in range(HEADS // 2):
        cols = slice(pair * 128, pair * 128 + 128)
        q, k, v = q_out[:, cols], k_out[:, cols], v_out[:, cols]
        mixed = jnp.zeros((tokens, 128), F32)
        for head in (2 * pair, 2 * pair + 1):
            keep = pair_lanes(tokens, head)
            scores = dot(jnp.where(keep, q, jnp.zeros_like(q)), k, 1, 1) * scale
            scores = jnp.where(valid, scores, -1e30)
            top = jnp.max(scores, axis=-1, keepdims=True)
            exponent = jnp.exp(scores - top)
            total = jnp.sum(exponent, axis=-1, keepdims=True)
            weights = (exponent / total).astype(BF16)
            mixed = mixed + dot(weights, jnp.where(keep, v, jnp.zeros_like(v)))
            log_totals = jnp.where(head_lanes == head, top + jnp.log(total), log_totals)
        m_out[:, cols] = mixed.astype(BF16)
    lse_out[...] = log_totals
    middle = x + dot(m_out[...], full_ref[3]) + lane[5:6]
    middle_out[...] = middle
    scaled, _ = standardize(middle)
    normed = (scaled * lane[1:2] + lane[6:7]).astype(BF16)
    logits = dot(normed, router_ref[...], 1, 1) + rbias_ref[...]
    exponent = jnp.exp(logits - jnp.max(logits, axis=-1, keepdims=True))
    probs = exponent / jnp.sum(exponent, axis=-1, keepdims=True)
    probs_out[...] = probs
    gates = [
        jnp.sum(expert_hot(routes_ref[...], experts, j) * probs, axis=-1, keepdims=True)
        for j in range(2)
    ]
    for j in range(2):
        gates_out[:, j : j + 1] = gates[j]
    rows = send_out.shape[0]
    picks = [slot_rows(row_ref[...], rows, j) for j in range(2)]
    send_out[:, :width] = dot(picks[0] + picks[1], normed).astype(BF16)
    if not first:
        cot = cot_ref[...]
        sent = sum(dot(picks[j], (gates[j] * cot).astype(BF16)) for j in range(2))
        send_out[:, width:] = sent.astype(BF16)


def mixer_backward_body(last, count, scale, experts, *refs):
    (
        g_ref,
        back_ref,
        x_ref,
        middle_ref,
        q_ref,
        k_ref,
        v_ref,
        m_ref,
        lse_ref,
        probs_ref,
        gates_ref,
        routes_ref,
        targets_ref,
        here_ref,
        full_ref,
        lane_ref,
        router_ref,
    ) = refs[:17]
    if last:
        row_prev_ref, gates_prev_ref, g_out, keep_out, give_out, small_out = refs[17:23]
        act_out, send_out = refs[23:25]
        dq_ref, dk_ref, dv_ref, dm_ref = refs[25:]
        y_back, d_back = back_ref[:, : g_ref.shape[1]], back_ref[:, g_ref.shape[1] :]
    else:
        y_ref, g_out, keep_out, give_out, small_out = refs[17:22]
        dq_ref, dk_ref, dv_ref, dm_ref = refs[22:]
        y_back, d_back = y_ref[...], back_ref[...]
    tokens, width = g_ref.shape
    rows = y_back.shape[0]
    lane = lane_ref[...]
    g = g_ref[...]
    middle = middle_ref[...]
    picks = [slot_columns(targets_ref[...], rows, j) for j in range(2)]
    dprobs = jnp.zeros((tokens, experts), F32)
    added = middle
    for j in range(2):
        picked = dot(picks[j], y_back)
        if last:
            added = added + gates_ref[:, j : j + 1] * picked
        dgate = jnp.sum(g * picked, axis=-1, keepdims=True)
        dprobs = dprobs + expert_hot(routes_ref[...], experts, j) * dgate
    if last:
        act_out[...] = added.astype(BF16)
    probs = probs_ref[...]
    dz = (probs * (dprobs - jnp.sum(dprobs * probs, axis=-1, keepdims=True))).astype(BF16)
    scaled, inverse = standardize(middle)
    normed = (scaled * lane[1:2] + lane[6:7]).astype(BF16)
    small_out[7 : 7 + experts, :] = dot(dz, normed, 0, 0)
    rbias_grad = jnp.sum(dz.astype(F32), axis=0, keepdims=True)
    small_out[7 + experts :, :] = jnp.zeros((small_out.shape[0] - 7 - experts, width), F32)
    small_out[7 + experts : 8 + experts, :experts] = rbias_grad
    dn = dot(dz, router_ref[...]) + dot(picks[0] + picks[1], d_back)
    dmiddle, gain_second, shift_second = norm_backward(dn, scaled, inverse, lane[1:2])
    dmiddle = dmiddle + g
    small_out[1:2, :] = gain_second
    small_out[6:7, :] = shift_second
    small_out[5:6, :] = jnp.sum(dmiddle, axis=0, keepdims=True)
    branch = dmiddle.astype(BF16)
    parts = keep_out.shape[0]
    part = width // parts
    core = here_ref[1]

    def store_dense(which, value):
        def store(target):
            for f in range(parts):
                target[f, which % 2] = value[f * part : (f + 1) * part, :].astype(BF16)

        pl.when(core == which // 2)(lambda: store(keep_out))
        pl.when(core != which // 2)(lambda: store(give_out))

    store_dense(3, dot(m_ref[...], branch, 0, 0))
    dm_ref[...] = dot(branch, full_ref[3], 1, 1).astype(BF16)
    valid = lax.broadcasted_iota(jnp.int32, (tokens, tokens), 1) < count
    for pair in range(HEADS // 2):
        cols = slice(pair * 128, pair * 128 + 128)
        q, k, v, dm = q_ref[:, cols], k_ref[:, cols], v_ref[:, cols], dm_ref[:, cols]
        dq = jnp.zeros((tokens, 128), F32)
        dk = jnp.zeros((tokens, 128), F32)
        dv = jnp.zeros((tokens, 128), F32)
        zero = jnp.zeros_like(q)
        for head in (2 * pair, 2 * pair + 1):
            keep = pair_lanes(tokens, head)
            q_one, k_one = jnp.where(keep, q, zero), jnp.where(keep, k, zero)
            dm_one = jnp.where(keep, dm, zero)
            scores = dot(q_one, k, 1, 1) * scale
            weights = jnp.where(
                valid, jnp.exp(scores - lse_ref[:, head : head + 1]), 0.0
            )
            dv = dv + dot(weights.astype(BF16), dm_one, 0, 0)
            dp = dot(dm_one, v, 1, 1)
            ds = weights * (dp - jnp.sum(dp * weights, axis=-1, keepdims=True))
            ds = ds.astype(BF16)
            dq = dq + dot(ds, k_one)
            dk = dk + dot(ds, q_one, 0, 0)
        dq_ref[:, cols] = (dq * scale).astype(BF16)
        dk_ref[:, cols] = (dk * scale).astype(BF16)
        dv_ref[:, cols] = dv.astype(BF16)
    small_out[3:4, :] = jnp.sum(dq_ref[...].astype(F32), axis=0, keepdims=True)
    small_out[4:5, :] = jnp.sum(dv_ref[...].astype(F32), axis=0, keepdims=True)
    scaled, inverse = standardize(x_ref[...])
    normed = (scaled * lane[0:1] + lane[2:3]).astype(BF16)
    dn = jnp.zeros((tokens, width), F32)
    for i, ref in enumerate((dq_ref, dk_ref, dv_ref)):
        store_dense(i, dot(normed, ref[...], 0, 0))
        dn = dn + dot(ref[...], full_ref[i], 1, 1)
    dx, gain_first, shift_first = norm_backward(dn, scaled, inverse, lane[0:1])
    small_out[0:1, :] = gain_first
    small_out[2:3, :] = shift_first
    dx = dx + dmiddle
    g_out[...] = dx
    if last:
        sent = sum(
            dot(
                slot_rows(row_prev_ref[...], send_out.shape[0], j),
                (gates_prev_ref[:, j : j + 1] * dx).astype(BF16),
            )
            for j in range(2)
        )
        send_out[...] = sent.astype(BF16)


CHUNK = 256
BLOCK = 256


def expert_pieces(rows, grads, pieces, biases, slopes, total, back, outs, finish):
    count, width = (grads if rows is None else rows).shape
    part = pieces[0][0].shape[1]
    forward, backward = rows is not None, grads is not None
    keep = forward and not backward
    operands, names = [], []

    def give(name, value):
        if value is not None:
            names.append(name)
            operands.append(value)

    give("rows", rows)
    give("grads", grads)
    for i, (weight_in, weight_out) in enumerate(pieces):
        give(("in", i), weight_in)
        give(("out", i), weight_out)
    give("biases", biases)
    give("slopes", slopes)
    give("total", total)
    give("back", back)
    kind = BF16 if finish else F32
    shapes = []
    if forward and backward:
        shapes.append(("both", shaped((count, 2 * width), kind)))
    elif forward:
        shapes.append(("y", shaped((count, width), kind)))
        shapes.append(("kept", shaped((len(pieces), count, part), BF16)))
    else:
        shapes.append(("d", shaped((count, width), kind)))
    scratch = [pltpu.VMEM((count, width), F32)] * (forward + backward)

    def body(*refs):
        at = dict(zip(names + [n for n, _ in shapes], refs))
        sums = list(refs[len(names) + len(shapes) :])
        y_sum = sums.pop(0) if forward else None
        d_sum = sums.pop(0) if backward else None
        if forward:
            y_sum[...] = at["total"][...] if "total" in at else jnp.zeros_like(y_sum)
        if backward:
            d_sum[...] = at["back"][...] if "back" in at else jnp.zeros_like(d_sum)
        for i in range(len(pieces)):

            def step(c, carry):
                cols = pl.ds(pl.multiple_of(c * CHUNK, CHUNK), CHUNK)
                weight_in, weight_out = at["in", i][:, cols], at["out", i][cols, :]
                for start in range(0, count, BLOCK):
                    here = slice(start, start + BLOCK)
                    if forward:
                        pre = dot(at["rows"][here, :], weight_in) + at["biases"][i : i + 1, cols]
                        active, slope = gelu_both(pre)
                        y_sum[here, :] += dot(active.astype(BF16), weight_out)
                        if keep:
                            at["kept"][i, here, cols] = slope.astype(BF16)
                    else:
                        slope = at["slopes"][i, here, cols].astype(F32)
                    if backward:
                        grad = dot(at["grads"][here, :], weight_out, 1, 1)
                        d_sum[here, :] += dot((grad * slope).astype(BF16), weight_in, 1, 1)
                return carry

            lax.fori_loop(0, part // CHUNK, step, 0)
        if forward and backward:
            at["both"][:, :width] = y_sum[...].astype(kind)
            at["both"][:, width:] = d_sum[...].astype(kind)
        elif forward:
            at["y"][...] = y_sum[...].astype(kind)
        else:
            at["d"][...] = d_sum[...].astype(kind)

    return pl.pallas_call(
        body,
        out_shape=[s for _, s in shapes],
        scratch_shapes=scratch,
        compiler_params=pltpu.CompilerParams(vmem_limit_bytes=VMEM_LIMIT),
        cost_estimate=pl.CostEstimate(
            flops=4 * (forward + backward) * count * width * part * len(pieces),
            bytes_accessed=20_000_000,
            transcendentals=0,
        ),
    )(*operands)


def expert_grads(rows, grads, weight_in, bias_column, weight_out):
    pieces = len(rows)
    count, width = rows[0].shape
    part = weight_in.shape[1]

    def body(*refs):
        rows_refs, grads_refs = refs[:pieces], refs[pieces : 2 * pieces]
        in_ref, bias_ref, out_ref, in_out, bias_out, w_out, sum_out, turned, total = refs[
            2 * pieces :
        ]
        turned[...] = in_ref[...].astype(F32).T.astype(BF16)

        def step(c, carry):
            here = pl.ds(pl.multiple_of(c * CHUNK, CHUNK), CHUNK)
            weight_grad = jnp.zeros((CHUNK, width), F32)
            turned_grad = jnp.zeros((CHUNK, width), F32)
            bias_grad = jnp.zeros((CHUNK, 1), F32)
            for rows_ref, grads_ref in zip(rows_refs, grads_refs):
                pre = dot(turned[here, :], rows_ref[...], 1, 1) + bias_ref[here, :]
                active, slope = gelu_both(pre)
                weight_grad += dot(active.astype(BF16), grads_ref[...])
                grad = (dot(out_ref[here, :], grads_ref[...], 1, 1) * slope).astype(BF16)
                bias_grad += jnp.sum(grad.astype(F32), axis=1, keepdims=True)
                turned_grad += dot(grad, rows_ref[...])
            w_out[here, :] = weight_grad
            total[here, :] = turned_grad
            bias_out[here, :] = bias_grad
            return carry

        lax.fori_loop(0, part // CHUNK, step, 0)
        sum_out[...] = sum(
            jnp.sum(ref[...].astype(F32), axis=0, keepdims=True) for ref in grads_refs
        )
        in_out[...] = total[...].T

    return pl.pallas_call(
        body,
        out_shape=(
            shaped((width, part), F32),
            shaped((part, 1), F32),
            shaped((part, width), F32),
            shaped((1, width), F32),
        ),
        scratch_shapes=[pltpu.VMEM((part, width), BF16), pltpu.VMEM((part, width), F32)],
        compiler_params=pltpu.CompilerParams(vmem_limit_bytes=VMEM_LIMIT),
        cost_estimate=pl.CostEstimate(
            flops=8 * pieces * count * width * part, bytes_accessed=20_000_000, transcendentals=0
        ),
    )(*rows, *grads, weight_in, bias_column, weight_out)


def ahead(value, steps, axis="fsdp"):
    size = lax.axis_size(axis)
    return lax.ppermute(value, axis, [((i + steps) % size, i) for i in range(size)])


def other_core(value):
    size = lax.axis_size("expert")
    return lax.ppermute(value, "expert", [(i ^ 1, i) for i in range(size)])


def ring_pair(first, second):
    next_first, next_second = ahead(first, 1), ahead(second, 1)
    last_first, last_second = ahead(first, 3), ahead(second, 3)
    far_first, far_second = ahead(next_first, 1), ahead(last_second, 3)
    return [
        (first, second),
        (next_first, next_second),
        (far_first, far_second),
        (last_first, last_second),
    ]


def ring_weights(packed, core):
    half = lax.dynamic_slice_in_dim(packed, 2 * core, 2, axis=0)
    after, before = ahead(half, 1), ahead(half, 3)
    far = jnp.concatenate([ahead(after[0:1], 1), ahead(before[1:2], 3)], axis=0)
    mine = [after, far, before]
    return [packed] + mine + [other_core(a) for a in mine]


def swap(rows, stride):
    width = rows.shape[-1]
    moved = lax.all_to_all(
        rows.reshape(-1, stride, width), "expert", split_axis=0, concat_axis=0, tiled=True
    )
    return moved.reshape(-1, width)


def pack_small(norm_gain, mixer_bias, router_weight, router_bias, expert_in_bias):
    part = norm_gain.shape[-1]
    lanes = jnp.concatenate([norm_gain, mixer_bias], axis=1)
    return jnp.concatenate(
        [
            lanes.reshape(-1, part),
            jnp.swapaxes(router_weight, 1, 2).reshape(-1, part),
            jnp.pad(router_bias, ((0, 0), (0, part - router_bias.shape[1]))),
            expert_in_bias.reshape(-1, part),
        ],
        axis=0,
    )


def shards(
    tokens,
    qkv_weight,
    out_weight,
    norm_gain,
    mixer_bias,
    router_weight,
    router_bias,
    expert_in,
    expert_in_bias,
    expert_out,
    expert_out_bias,
    routes,
    cotangent,
):
    count, width = tokens.shape
    parts = lax.axis_size("fsdp")
    experts = lax.axis_size("expert") * expert_in.shape[1]
    capacity = max(2, (3 * count + experts - 1) // experts)
    stride = -(-capacity // 8) * 8
    rows = experts * stride
    held = -(-count // 16) * 16
    part = width // parts
    scale = (width // HEADS) ** (-0.5)
    gather = lambda a: lax.all_gather(a, "fsdp", axis=0, tiled=False)
    fill = ((0, held - count), (0, 0))

    small_all = gather(
        pack_small(norm_gain, mixer_bias, router_weight, router_bias, expert_in_bias)
    )
    at_router = 7 * LAYERS
    at_rbias = at_router + LAYERS * experts
    at_ebias = at_rbias + LAYERS
    lanes = jnp.swapaxes(small_all[:, :at_rbias], 0, 1).reshape(at_rbias, width)
    lane_rows = lanes[:at_router].astype(F32).reshape(LAYERS, 7, width)
    routers = lanes[at_router:].reshape(LAYERS, experts, width)
    rbias = small_all[:, at_rbias:at_ebias, : router_bias.shape[1]]
    rbias = jnp.swapaxes(rbias, 0, 1).reshape(LAYERS, 1, experts).astype(F32)
    ebias = small_all[:, at_ebias:].reshape(parts, LAYERS, -1).astype(F32)

    me, core = lax.axis_index("fsdp"), lax.axis_index("expert") % 2
    here = jnp.stack([me, core]).astype(jnp.int32)
    packed = [
        jnp.concatenate([qkv_weight[layer], out_weight[layer][None]], axis=0)
        for layer in range(LAYERS)
    ]
    weights0 = ring_weights(packed[0], core)
    wide0 = ring_pair(expert_in[0, 0], expert_out[0, 0])
    weights1 = ring_weights(packed[1], core)
    wide1 = ring_pair(expert_in[1, 0], expert_out[1, 0])
    order = (me + jnp.arange(parts)) % parts
    hidden_bias = [jnp.take(ebias[:, layer], order, axis=0) for layer in range(LAYERS)]
    targets = [
        jnp.pad(slot_targets(routes[layer], experts, stride), fill, constant_values=-1)
        for layer in range(LAYERS)
    ]
    turned = [a.T for a in targets]
    named = [jnp.pad(routes[layer], fill) for layer in range(LAYERS)]
    bias_out = [expert_out_bias[layer].astype(F32) for layer in range(LAYERS)]
    x0 = jnp.pad(tokens, fill).astype(F32)
    cot = jnp.pad(cotangent, fill).astype(F32)

    kept_shapes = [shaped((held, width), BF16)] * 4 + [
        shaped((held, 128), F32),
        shaped((held, experts), F32),
        shaped((held, 2), F32),
    ]
    full_rows = shaped((held, width), F32)

    full_shape = shaped((4, width, width), BF16)

    def mixer_forward(first, args, outs):
        return pl.pallas_call(
            functools.partial(mixer_forward_body, first, count, scale, experts),
            out_shape=outs + [full_shape],
            in_specs=[pl.BlockSpec(memory_space=pltpu.SMEM)]
            + [pl.BlockSpec(memory_space=pltpu.VMEM)] * (len(args) - 1),
            compiler_params=pltpu.CompilerParams(vmem_limit_bytes=VMEM_LIMIT),
            cost_estimate=pl.CostEstimate(
                flops=2_000_000_000, bytes_accessed=20_000_000, transcendentals=0
            ),
        )(*args)

    middle0, send, *kept0 = mixer_forward(
        True,
        (here, *weights0, x0, lane_rows[0], routers[0], rbias[0], named[0], turned[0]),
        [full_rows, shaped((rows, width), BF16)] + kept_shapes,
    )
    full0 = kept0.pop()
    rows0 = swap(send, stride)
    near = [wide0[0], wide0[1], wide0[3]]
    near_bias = jnp.stack([hidden_bias[0][0], hidden_bias[0][1], hidden_bias[0][3]])
    start = jnp.broadcast_to(bias_out[0], (rows, width))
    total, near_slopes = expert_pieces(
        rows0, None, near, near_bias, None, start, None, None, False
    )
    result, far_slopes = expert_pieces(
        rows0, None, [wide0[2]], hidden_bias[0][2:3], None, total, None, None, True
    )
    y0 = swap(result, stride)
    gates0 = kept0[6]
    middle1, send, *kept1 = mixer_forward(
        False,
        (here, *weights1, middle0, y0, gates0, targets[0], cot)
        + (lane_rows[1], routers[1], rbias[1], named[1], turned[1]),
        [full_rows, shaped((rows, 2 * width), BF16)] + kept_shapes + [full_rows],
    )
    full1 = kept1.pop()
    x1 = kept1.pop()
    both = swap(send, stride)
    rows1, grads1 = both[:, :width], both[:, width:]
    start = jnp.broadcast_to(bias_out[1], (rows, width))
    (both,) = expert_pieces(
        rows1, grads1, wide1, hidden_bias[1], None, start, None, None, True
    )
    both = swap(both, stride)

    half_shape = shaped((parts, 2, part, width), BF16)
    small_shape = shaped((40, width), F32)
    scratch = [pltpu.VMEM((held, width), BF16)] * 4

    def mixer_backward(last, args, outs):
        specs = [pl.BlockSpec(memory_space=pltpu.VMEM)] * len(args)
        specs[13] = pl.BlockSpec(memory_space=pltpu.SMEM)
        return pl.pallas_call(
            functools.partial(mixer_backward_body, last, count, scale, experts),
            out_shape=outs,
            in_specs=specs,
            scratch_shapes=scratch,
            compiler_params=pltpu.CompilerParams(vmem_limit_bytes=VMEM_LIMIT),
            cost_estimate=pl.CostEstimate(
                flops=4_000_000_000, bytes_accessed=20_000_000, transcendentals=0
            ),
        )(*args)

    q, k, v, m, lse, probs, gates = kept1
    g, keep1, give1, small1, activations, send = mixer_backward(
        True,
        (cot, both, x1, middle1, q, k, v, m, lse, probs, gates, named[1], targets[1])
        + (here, full1, lane_rows[1], routers[1], turned[0], gates0),
        [
            full_rows,
            half_shape,
            half_shape,
            small_shape,
            shaped((held, width), BF16),
            shaped((rows, width), BF16),
        ],
    )
    grads0 = swap(send, stride)
    near_back = expert_pieces(
        None,
        grads0,
        near + [wide0[2]],
        None,
        jnp.concatenate([near_slopes, far_slopes]),
        None,
        None,
        None,
        True,
    )
    back0 = swap(near_back[0], stride)
    q, k, v, m, lse, probs, gates = kept0
    g, keep0, give0, small0 = mixer_backward(
        False,
        (g, back0, x0, middle0, q, k, v, m, lse, probs, gates, named[0], targets[0])
        + (here, full0, lane_rows[0], routers[0], y0),
        [full_rows, half_shape, half_shape, small_shape],
    )

    size = lax.axis_size("expert")
    same_core = [[i for i in range(size) if i % 2 == c] for c in range(2)]

    def reduce_dense(keep, give, more=None):
        chip = (keep.astype(F32) + other_core(give).astype(F32)).astype(BF16)
        chip = chip.reshape(parts, 2 * part, width)
        if more is not None:
            extra = more.shape[0] // 2
            paired = more.astype(BF16).reshape(2, extra, width)
            mine = lax.dynamic_index_in_dim(paired, core, 0, keepdims=False).astype(F32)
            theirs = lax.dynamic_index_in_dim(paired, 1 - core, 0, keepdims=False)
            mine = (mine + other_core(theirs).astype(F32)).astype(BF16)
            chip = jnp.concatenate(
                [chip, jnp.broadcast_to(mine[None], (parts, extra, width))], axis=1
            )
        lines = chip.shape[1]
        got = lax.all_to_all(chip, "fsdp", split_axis=0, concat_axis=0, tiled=True)
        summed = jnp.sum(got.astype(F32), axis=0).astype(BF16)
        each = 2 * lines // size
        got = lax.all_to_all(
            summed.reshape(size // 2, each, width),
            "expert",
            split_axis=0,
            concat_axis=0,
            tiled=True,
            axis_index_groups=same_core,
        )
        final = jnp.sum(got.astype(F32), axis=0).astype(BF16)
        got = lax.all_to_all(
            jnp.broadcast_to(final[None], (size, each, width)),
            "expert",
            split_axis=0,
            concat_axis=0,
            tiled=True,
        )
        got = got.reshape(size // 2, 2, each, width).swapaxes(0, 1).reshape(2, lines, width)
        return got[:, : 2 * part].reshape(4, part, width), got[:, 2 * part :].reshape(-1, width)

    def own_grads(layer, pieces):
        a, b, c, d = expert_grads(
            [p[0] for p in pieces],
            [p[1] for p in pieces],
            expert_in[layer, 0],
            expert_in_bias[layer, 0].astype(F32)[:, None],
            expert_out[layer, 0],
        )
        return a, b[:, 0], c, d[0]

    own1 = own_grads(1, ring_pair(rows1, grads1))
    own0 = own_grads(0, ring_pair(rows0, grads0))
    dense1, _ = reduce_dense(keep1, give1)
    smalls = jnp.concatenate([small0, small1, jnp.zeros((-80 % size, width), F32)])
    dense0, smalls = reduce_dense(keep0, give0, smalls)
    dense_sum = jnp.stack([dense0, dense1]).astype(F32)
    small_sum = smalls[:80].astype(F32).reshape(LAYERS, 40, width)
    mine = lax.dynamic_slice_in_dim(small_sum, me * part, part, axis=2)
    router_grad = jnp.swapaxes(mine[:, 7 : 7 + experts], 1, 2)
    rbias_grad = lax.dynamic_slice_in_dim(
        small_sum[:, 7 + experts], me * router_bias.shape[1], router_bias.shape[1], axis=1
    )
    in_grad, in_bias_grad, out_grad, out_bias_grad = (
        jnp.stack([a, b])[:, None] for a, b in zip(own0, own1)
    )
    return (
        activations[:count],
        g[:count],
        dense_sum[:, :3],
        dense_sum[:, 3],
        mine[:, :2],
        mine[:, 2:7],
        router_grad,
        rbias_grad,
        in_grad,
        in_bias_grad,
        out_grad,
        out_bias_grad,
    )


def solution(mesh):
    tokens_spec = P(("expert", "fsdp"), None)
    params = (
        P(None, None, "fsdp", None),
        P(None, "fsdp", None),
        P(None, None, "fsdp"),
        P(None, None, "fsdp"),
        P(None, "fsdp", None),
        P(None, "fsdp"),
        P(None, "expert", None, "fsdp"),
        P(None, "expert", "fsdp"),
        P(None, "expert", "fsdp", None),
        P(None, "expert", None),
    )
    return jax.shard_map(
        shards,
        mesh=mesh,
        in_specs=(tokens_spec,) + params + (P(None, ("expert", "fsdp"), None), tokens_spec),
        out_specs=(tokens_spec, tokens_spec) + params,
        check_vma=False,
    )
```

```python
import functools

import jax
import jax.numpy as jnp
from jax import lax
from jax.experimental import pallas as pl
from jax.experimental.pallas import tpu as pltpu
from jax.sharding import PartitionSpec as P

HEADS = 12
LAYERS = 2
EPSILON = 1e-06
BF16 = jnp.bfloat16
F32 = jnp.float32
VMEM_LIMIT = 56 * 1024 * 1024


def dot(left, right, left_dim=1, right_dim=0):
    return lax.dot_general(
        left, right, (((left_dim,), (right_dim,)), ((), ())), preferred_element_type=F32
    )


def shaped(shape, kind):
    return jax.ShapeDtypeStruct(shape, kind)


def standardize(values):
    centred = values - jnp.mean(values, axis=-1, keepdims=True)
    inverse = lax.rsqrt(jnp.mean(centred * centred, axis=-1, keepdims=True) + EPSILON)
    return centred * inverse, inverse


def norm_backward(grad_out, scaled, inverse, gain):
    grad_scaled = grad_out * gain
    mean_grad = jnp.mean(grad_scaled, axis=-1, keepdims=True)
    mean_cross = jnp.mean(grad_scaled * scaled, axis=-1, keepdims=True)
    grad_input = inverse * (grad_scaled - mean_grad - scaled * mean_cross)
    return (
        grad_input,
        jnp.sum(grad_out * scaled, axis=0, keepdims=True),
        jnp.sum(grad_out, axis=0, keepdims=True),
    )


def gelu_both(pre):
    cdf = 0.5 + 0.5 * lax.erf(pre * (0.5**0.5))
    bell = jnp.exp2(pre * pre * (-0.5 * 1.4426950408889634))
    return pre * cdf, cdf + pre * (bell * 0.3989422804014327)


class Fetch:
    def __init__(self, sources, targets, semaphores):
        self.copies = [
            pltpu.make_async_copy(source, target, semaphores.at[i])
            for i, (source, target) in enumerate(zip(sources, targets))
        ]
        for copy in self.copies:
            copy.start()

    def wait(self, *which):
        for i in which:
            self.copies[i].wait()


def slot_targets(routes_layer, experts, stride):
    flat = routes_layer.reshape(-1)
    count = flat.shape[0]
    onehot = (flat[:, None] == jnp.arange(experts, dtype=jnp.int32)[None, :]).astype(BF16)
    below = (jnp.arange(count)[None, :] < jnp.arange(count)[:, None]).astype(BF16)
    earlier = dot(below, onehot)
    position = jnp.sum(earlier * onehot.astype(F32), axis=1).astype(jnp.int32)
    return (flat * stride + position).reshape(-1, 2)


def slot_rows(targets_row, rows, which):
    tokens = targets_row.shape[1]
    slots = lax.broadcasted_iota(jnp.int32, (rows, tokens), 0)
    return (slots == targets_row[which : which + 1, :]).astype(F32).astype(BF16)


def slot_columns(targets, rows, which):
    tokens = targets.shape[0]
    slots = lax.broadcasted_iota(jnp.int32, (tokens, rows), 1)
    return (slots == targets[:, which : which + 1]).astype(F32).astype(BF16)


def expert_hot(routes, experts, which):
    places = lax.broadcasted_iota(jnp.int32, (routes.shape[0], experts), 1)
    return (places == routes[:, which : which + 1]).astype(F32)


def pair_lanes(tokens, head):
    lanes = lax.broadcasted_iota(jnp.int32, (tokens, 128), 1)
    return (lanes // 64) == head % 2


def place_weights(here_ref, own_ref, mine, theirs, full_ref):
    _, part, _ = own_ref.shape
    parts = full_ref.shape[1] // part
    me, core = here_ref[0], here_ref[1]

    def spot(ahead):
        return pl.ds(pl.multiple_of(lax.rem(me + ahead, parts) * part, part), part)

    for kind in range(4):
        full_ref[kind, spot(0), :] = own_ref[kind]
    for ahead, (mine_ref, theirs_ref) in enumerate(zip(mine, theirs), start=1):
        for half in range(2):
            full_ref[2 * core + half, spot(ahead), :] = mine_ref[half]
            full_ref[2 * (1 - core) + half, spot(ahead), :] = theirs_ref[half]


def mixer_forward_body(first, count, scale, experts, *refs):
    here_ref, own_ref = refs[:2]
    full_ref = refs[-1]
    place_weights(here_ref, own_ref, refs[2:5], refs[5:8], full_ref)
    refs = refs[8:-1]
    if first:
        (x_ref, lane_ref, router_ref, rbias_ref, routes_ref, row_ref) = refs[:6]
        outs = refs[6:]
        x = x_ref[...]
    else:
        (
            middle_ref,
            back_ref,
            gates_prev_ref,
            targets_prev_ref,
            cot_ref,
            lane_ref,
            router_ref,
            rbias_ref,
            routes_ref,
            row_ref,
        ) = refs[:10]
        outs = refs[10:]
        x = middle_ref[...]
        back = back_ref[...]
        for j in range(2):
            picked = dot(slot_columns(targets_prev_ref[...], back.shape[0], j), back)
            x = x + gates_prev_ref[:, j : j + 1] * picked
    middle_out, send_out, q_out, k_out, v_out, m_out, lse_out, probs_out, gates_out = outs[:9]
    if not first:
        outs[9][...] = x
    tokens, width = x.shape
    lane = lane_ref[...]
    scaled, _ = standardize(x)
    normed = (scaled * lane[0:1] + lane[2:3]).astype(BF16)
    q_out[...] = (dot(normed, full_ref[0]) + lane[3:4]).astype(BF16)
    k_out[...] = dot(normed, full_ref[1]).astype(BF16)
    v_out[...] = (dot(normed, full_ref[2]) + lane[4:5]).astype(BF16)
    valid = lax.broadcasted_iota(jnp.int32, (tokens, tokens), 1) < count
    log_totals = jnp.zeros((tokens, 128), F32)
    head_lanes = lax.broadcasted_iota(jnp.int32, (tokens, 128), 1)
    for pair in range(HEADS // 2):
        cols = slice(pair * 128, pair * 128 + 128)
        q, k, v = q_out[:, cols], k_out[:, cols], v_out[:, cols]
        mixed = jnp.zeros((tokens, 128), F32)
        for head in (2 * pair, 2 * pair + 1):
            keep = pair_lanes(tokens, head)
            scores = dot(jnp.where(keep, q, jnp.zeros_like(q)), k, 1, 1) * scale
            scores = jnp.where(valid, scores, -1e30)
            top = jnp.max(scores, axis=-1, keepdims=True)
            exponent = jnp.exp(scores - top)
            total = jnp.sum(exponent, axis=-1, keepdims=True)
            weights = (exponent / total).astype(BF16)
            mixed = mixed + dot(weights, jnp.where(keep, v, jnp.zeros_like(v)))
            log_totals = jnp.where(head_lanes == head, top + jnp.log(total), log_totals)
        m_out[:, cols] = mixed.astype(BF16)
    lse_out[...] = log_totals
    middle = x + dot(m_out[...], full_ref[3]) + lane[5:6]
    middle_out[...] = middle
    scaled, _ = standardize(middle)
    normed = (scaled * lane[1:2] + lane[6:7]).astype(BF16)
    logits = dot(normed, router_ref[...], 1, 1) + rbias_ref[...]
    exponent = jnp.exp(logits - jnp.max(logits, axis=-1, keepdims=True))
    probs = exponent / jnp.sum(exponent, axis=-1, keepdims=True)
    probs_out[...] = probs
    gates = [
        jnp.sum(expert_hot(routes_ref[...], experts, j) * probs, axis=-1, keepdims=True)
        for j in range(2)
    ]
    for j in range(2):
        gates_out[:, j : j + 1] = gates[j]
    rows = send_out.shape[0]
    picks = [slot_rows(row_ref[...], rows, j) for j in range(2)]
    send_out[:, :width] = dot(picks[0] + picks[1], normed).astype(BF16)
    if not first:
        cot = cot_ref[...]
        sent = sum(dot(picks[j], (gates[j] * cot).astype(BF16)) for j in range(2))
        send_out[:, width:] = sent.astype(BF16)


def mixer_backward_body(last, count, scale, experts, *refs):
    (
        g_ref,
        back_ref,
        x_ref,
        middle_ref,
        q_ref,
        k_ref,
        v_ref,
        m_ref,
        lse_ref,
        probs_ref,
        gates_ref,
        routes_ref,
        targets_ref,
        here_ref,
        full_ref,
        lane_ref,
        router_ref,
    ) = refs[:17]
    if last:
        row_prev_ref, gates_prev_ref, g_out, keep_out, give_out, small_out = refs[17:23]
        act_out, send_out = refs[23:25]
        dq_ref, dk_ref, dv_ref, dm_ref = refs[25:]
        y_back, d_back = back_ref[:, : g_ref.shape[1]], back_ref[:, g_ref.shape[1] :]
    else:
        y_ref, g_out, keep_out, give_out, small_out = refs[17:22]
        dq_ref, dk_ref, dv_ref, dm_ref = refs[22:]
        y_back, d_back = y_ref[...], back_ref[...]
    tokens, width = g_ref.shape
    rows = y_back.shape[0]
    lane = lane_ref[...]
    g = g_ref[...]
    middle = middle_ref[...]
    picks = [slot_columns(targets_ref[...], rows, j) for j in range(2)]
    dprobs = jnp.zeros((tokens, experts), F32)
    added = middle
    for j in range(2):
        picked = dot(picks[j], y_back)
        if last:
            added = added + gates_ref[:, j : j + 1] * picked
        dgate = jnp.sum(g * picked, axis=-1, keepdims=True)
        dprobs = dprobs + expert_hot(routes_ref[...], experts, j) * dgate
    if last:
        act_out[...] = added.astype(BF16)
    probs = probs_ref[...]
    dz = (probs * (dprobs - jnp.sum(dprobs * probs, axis=-1, keepdims=True))).astype(BF16)
    scaled, inverse = standardize(middle)
    normed = (scaled * lane[1:2] + lane[6:7]).astype(BF16)
    small_out[7 : 7 + experts, :] = dot(dz, normed, 0, 0)
    rbias_grad = jnp.sum(dz.astype(F32), axis=0, keepdims=True)
    small_out[7 + experts :, :] = jnp.zeros((small_out.shape[0] - 7 - experts, width), F32)
    small_out[7 + experts : 8 + experts, :experts] = rbias_grad
    dn = dot(dz, router_ref[...]) + dot(picks[0] + picks[1], d_back)
    dmiddle, gain_second, shift_second = norm_backward(dn, scaled, inverse, lane[1:2])
    dmiddle = dmiddle + g
    small_out[1:2, :] = gain_second
    small_out[6:7, :] = shift_second
    small_out[5:6, :] = jnp.sum(dmiddle, axis=0, keepdims=True)
    branch = dmiddle.astype(BF16)
    parts = keep_out.shape[0]
    part = width // parts
    core = here_ref[1]

    def store_dense(which, value):
        def store(target):
            for f in range(parts):
                target[f, which % 2] = value[f * part : (f + 1) * part, :].astype(BF16)

        pl.when(core == which // 2)(lambda: store(keep_out))
        pl.when(core != which // 2)(lambda: store(give_out))

    store_dense(3, dot(m_ref[...], branch, 0, 0))
    dm_ref[...] = dot(branch, full_ref[3], 1, 1).astype(BF16)
    valid = lax.broadcasted_iota(jnp.int32, (tokens, tokens), 1) < count
    for pair in range(HEADS // 2):
        cols = slice(pair * 128, pair * 128 + 128)
        q, k, v, dm = q_ref[:, cols], k_ref[:, cols], v_ref[:, cols], dm_ref[:, cols]
        dq = jnp.zeros((tokens, 128), F32)
        dk = jnp.zeros((tokens, 128), F32)
        dv = jnp.zeros((tokens, 128), F32)
        zero = jnp.zeros_like(q)
        for head in (2 * pair, 2 * pair + 1):
            keep = pair_lanes(tokens, head)
            q_one, k_one = jnp.where(keep, q, zero), jnp.where(keep, k, zero)
            dm_one = jnp.where(keep, dm, zero)
            scores = dot(q_one, k, 1, 1) * scale
            weights = jnp.where(
                valid, jnp.exp(scores - lse_ref[:, head : head + 1]), 0.0
            )
            dv = dv + dot(weights.astype(BF16), dm_one, 0, 0)
            dp = dot(dm_one, v, 1, 1)
            ds = weights * (dp - jnp.sum(dp * weights, axis=-1, keepdims=True))
            ds = ds.astype(BF16)
            dq = dq + dot(ds, k_one)
            dk = dk + dot(ds, q_one, 0, 0)
        dq_ref[:, cols] = (dq * scale).astype(BF16)
        dk_ref[:, cols] = (dk * scale).astype(BF16)
        dv_ref[:, cols] = dv.astype(BF16)
    small_out[3:4, :] = jnp.sum(dq_ref[...].astype(F32), axis=0, keepdims=True)
    small_out[4:5, :] = jnp.sum(dv_ref[...].astype(F32), axis=0, keepdims=True)
    scaled, inverse = standardize(x_ref[...])
    normed = (scaled * lane[0:1] + lane[2:3]).astype(BF16)
    dn = jnp.zeros((tokens, width), F32)
    for i, ref in enumerate((dq_ref, dk_ref, dv_ref)):
        store_dense(i, dot(normed, ref[...], 0, 0))
        dn = dn + dot(ref[...], full_ref[i], 1, 1)
    dx, gain_first, shift_first = norm_backward(dn, scaled, inverse, lane[0:1])
    small_out[0:1, :] = gain_first
    small_out[2:3, :] = shift_first
    dx = dx + dmiddle
    g_out[...] = dx
    if last:
        sent = sum(
            dot(
                slot_rows(row_prev_ref[...], send_out.shape[0], j),
                (gates_prev_ref[:, j : j + 1] * dx).astype(BF16),
            )
            for j in range(2)
        )
        send_out[...] = sent.astype(BF16)


CHUNK = 768
BLOCK = 256
GRAD_CHUNK = 256


def expert_pieces(rows, grads, pieces, biases, slopes, total, finish):
    forward, backward = rows is not None, grads is not None
    count = (rows if forward else grads).shape[0]
    width, part = pieces[0][0].shape
    keep = forward and not backward
    plain = [("rows" if forward else "grads", rows if forward else grads)]
    if forward:
        plain += [("biases", biases), ("total", total)]
    fetched = [a for pair in pieces for a in pair]
    slopes = slopes or []
    spots = [(j, k) for j, value in enumerate(slopes) for k in range(value.shape[0])]
    kind = BF16 if finish else F32
    shapes = []
    if forward and backward:
        shapes.append(("both", shaped((count, 2 * width), kind)))
    elif forward:
        shapes.append(("y", shaped((count, width), kind)))
        shapes.append(("kept", shaped((len(pieces), count, part), BF16)))
    else:
        shapes.append(("d", shaped((count, width), kind)))
    held = [pltpu.VMEM(a.shape, BF16) for a in fetched]
    held += [pltpu.VMEM((count, part), BF16) for _ in spots]
    source, first = ("rows", width) if forward else ("grads", 0)
    ends = [len(plain), len(fetched), len(slopes), len(shapes), len(held)]

    def body(*refs):
        refs = list(refs)
        plain_refs, far_refs, slope_refs, out_refs, held_refs = [
            [refs.pop(0) for _ in range(n)] for n in ends
        ]
        at = dict(zip([n for n, _ in plain] + [n for n, _ in shapes], plain_refs + out_refs))
        semaphores = refs.pop()
        fetch = Fetch(
            far_refs + [slope_refs[j].at[k] for j, k in spots], held_refs, semaphores
        )
        y_sum = refs.pop(0) if forward else None
        d_sum = refs.pop(0) if backward else None
        if forward:
            y_sum[...] = jnp.broadcast_to(at["total"][...], y_sum.shape)
        if backward:
            d_sum[...] = jnp.zeros_like(d_sum)
        for i in range(len(pieces)):
            in_ref, out_ref = held_refs[2 * i], held_refs[2 * i + 1]
            fetch.wait(2 * i, 2 * i + 1)
            if spots:
                slope_ref = held_refs[2 * len(pieces) + i]
                fetch.wait(2 * len(pieces) + i)
            for c in range(0, part, CHUNK):
                cols = slice(c, c + CHUNK)
                for start in range(0, count, BLOCK):
                    here = slice(start, start + BLOCK)
                    if forward:
                        pre = dot(at["rows"][here, :width], in_ref[:, cols])
                        active, slope = gelu_both(pre + at["biases"][i : i + 1, cols])
                        y_sum[here, :] += dot(active.astype(BF16), out_ref[cols, :])
                        if not backward:
                            at["kept"][i, here, cols] = slope.astype(BF16)
                    else:
                        slope = slope_ref[here, cols].astype(F32)
                    if backward:
                        grad = dot(at[source][here, first : first + width], out_ref[cols, :], 1, 1)
                        d_sum[here, :] += dot(
                            (grad * slope).astype(BF16), in_ref[:, cols], 1, 1
                        )
        if forward and backward:
            at["both"][:, :width] = y_sum[...].astype(kind)
            at["both"][:, width:] = d_sum[...].astype(kind)
        elif forward:
            at["y"][...] = y_sum[...].astype(kind)
        else:
            at["d"][...] = d_sum[...].astype(kind)

    return pl.pallas_call(
        body,
        out_shape=[s for _, s in shapes],
        in_specs=[pl.BlockSpec(memory_space=pltpu.VMEM)] * len(plain)
        + [pl.BlockSpec(memory_space=pl.ANY)] * (len(fetched) + len(slopes)),
        scratch_shapes=held
        + [pltpu.VMEM((count, width), F32)] * (forward + backward)
        + [pltpu.SemaphoreType.DMA((len(held),))],
        compiler_params=pltpu.CompilerParams(vmem_limit_bytes=VMEM_LIMIT),
        cost_estimate=pl.CostEstimate(
            flops=4 * (forward + backward) * count * width * part * len(pieces),
            bytes_accessed=20_000_000,
            transcendentals=0,
        ),
    )(*[a for _, a in plain], *fetched, *slopes)


def expert_grads(pieces, weight_in, bias_column, weight_out, layer, others=()):
    joint = not isinstance(pieces[0], tuple)
    width, part = weight_in.shape
    operands = list(pieces) if joint else [a for pair in pieces for a in pair]
    held = len(operands)
    count = sum(a.shape[0] for a in operands) // (1 if joint else 2)

    def body(*refs):
        given, refs = refs[:held], refs[held:]
        in_ref, bias_ref, out_ref = refs[:3]
        in_out, bias_out, w_out, sum_out, turned, total, *here_refs = refs[3 + len(others) :]
        fetch = Fetch(given, here_refs[:-1], here_refs[-1])
        turned[...] = in_ref[...].astype(F32).T.astype(BF16)
        for i in range(held if joint else held // 2):
            if joint:
                fetch.wait(i)
                rows_ref, grads_ref = here_refs[i].at[:, :width], here_refs[i].at[:, width:]
            else:
                fetch.wait(2 * i, 2 * i + 1)
                rows_ref, grads_ref = here_refs[2 * i], here_refs[2 * i + 1]

            def add(ref, index, value):
                ref[index] = value if i == 0 else ref[index] + value

            for c in range(0, part, GRAD_CHUNK):
                here = slice(c, c + GRAD_CHUNK)
                pre = dot(turned[here, :], rows_ref[...], 1, 1) + bias_ref[here, :]
                active, slope = gelu_both(pre)
                add(w_out, (0, here), dot(active.astype(BF16), grads_ref[...]))
                grad = (dot(out_ref[here, :], grads_ref[...], 1, 1) * slope).astype(BF16)
                add(bias_out, (0, here), jnp.sum(grad.astype(F32), axis=1, keepdims=True))
                add(total, (here, slice(None)), dot(grad, rows_ref[...]))
            add(sum_out, 0, jnp.sum(grads_ref[...].astype(F32), axis=0, keepdims=True))
        in_out[0] = total[...].T

    shapes = [(width, part), (part, 1), (part, width), (1, width)]
    fixed = lambda a: pl.BlockSpec(a.shape, lambda i: (0,) * a.ndim)
    scratch = [pltpu.VMEM(a.shape, BF16) for a in operands]
    scratch.append(pltpu.SemaphoreType.DMA((len(operands),)))
    small = [weight_in, bias_column, weight_out]
    return pl.pallas_call(
        body,
        grid=(1,),
        in_specs=[pl.BlockSpec(memory_space=pl.ANY)] * held
        + [fixed(a) for a in small]
        + [pl.BlockSpec(memory_space=pl.ANY)] * len(others),
        out_specs=[pl.BlockSpec((1,) + a, lambda i: (layer, 0, 0)) for a in shapes],
        out_shape=[shaped((LAYERS,) + a, F32) for a in shapes],
        input_output_aliases={held + len(small) + i: i for i in range(len(others))},
        scratch_shapes=[pltpu.VMEM((part, width), BF16), pltpu.VMEM((part, width), F32)] + scratch,
        compiler_params=pltpu.CompilerParams(vmem_limit_bytes=VMEM_LIMIT),
        cost_estimate=pl.CostEstimate(
            flops=8 * count * width * part, bytes_accessed=20_000_000, transcendentals=0
        ),
    )(*operands, *small, *others)


def ahead(value, steps, axis="fsdp"):
    size = lax.axis_size(axis)
    return lax.ppermute(value, axis, [((i + steps) % size, i) for i in range(size)])


def other_core(value):
    size = lax.axis_size("expert")
    return lax.ppermute(value, "expert", [(i ^ 1, i) for i in range(size)])


def tie(*values):
    return lax.optimization_barrier(values)


def ring_rows(rows):
    half = rows.shape[0] // 2
    after, before = ahead(rows, 1), ahead(rows, 3)
    return after, before, lambda a, b: (ahead(a[:half], 1), ahead(b[half:], 3))


def half_weights(packed, core):
    return lax.dynamic_slice_in_dim(packed, 2 * core, 2, axis=0)


def far_weights(after, before):
    return jnp.concatenate([ahead(after[0:1], 1), ahead(before[1:2], 3)], axis=0)


def swap(rows, stride):
    width = rows.shape[-1]
    moved = lax.all_to_all(
        rows.reshape(-1, stride, width), "expert", split_axis=0, concat_axis=0, tiled=True
    )
    return moved.reshape(-1, width)


def pack_small(norm_gain, mixer_bias, router_weight, router_bias, expert_in_bias):
    part = norm_gain.shape[-1]
    lanes = jnp.concatenate([norm_gain, mixer_bias], axis=1)
    return jnp.concatenate(
        [
            lanes.reshape(-1, part),
            jnp.swapaxes(router_weight, 1, 2).reshape(-1, part),
            jnp.pad(router_bias, ((0, 0), (0, part - router_bias.shape[1]))),
            expert_in_bias.reshape(-1, part),
        ],
        axis=0,
    )


def shards(
    tokens,
    qkv_weight,
    out_weight,
    norm_gain,
    mixer_bias,
    router_weight,
    router_bias,
    expert_in,
    expert_in_bias,
    expert_out,
    expert_out_bias,
    routes,
    cotangent,
):
    count, width = tokens.shape
    parts = lax.axis_size("fsdp")
    experts = lax.axis_size("expert") * expert_in.shape[1]
    capacity = max(2, (3 * count + experts - 1) // experts)
    stride = -(-capacity // 8) * 8
    rows = experts * stride
    held = -(-count // 16) * 16
    part = width // parts
    scale = (width // HEADS) ** (-0.5)
    fill = ((0, held - count), (0, 0))

    small_local = pack_small(
        norm_gain, mixer_bias, router_weight, router_bias, expert_in_bias
    )
    small_all = lax.all_to_all(
        jnp.broadcast_to(small_local[None], (parts,) + small_local.shape),
        "fsdp",
        split_axis=0,
        concat_axis=0,
        tiled=True,
    )
    at_router = 7 * LAYERS
    at_rbias = at_router + LAYERS * experts
    at_ebias = at_rbias + LAYERS
    lanes = jnp.swapaxes(small_all[:, :at_rbias], 0, 1).reshape(at_rbias, width)
    lane_rows = lanes[:at_router].astype(F32).reshape(LAYERS, 7, width)
    routers = lanes[at_router:].reshape(LAYERS, experts, width)
    rbias = small_all[:, at_rbias:at_ebias, : router_bias.shape[1]]
    rbias = jnp.swapaxes(rbias, 0, 1).reshape(LAYERS, 1, experts).astype(F32)
    ebias = small_all[:, at_ebias:].reshape(parts, LAYERS, -1).astype(F32)

    me, core = lax.axis_index("fsdp"), lax.axis_index("expert") % 2
    here = jnp.stack([me, core]).astype(jnp.int32)
    packed = [
        jnp.concatenate([qkv_weight[layer], out_weight[layer][None]], axis=0)
        for layer in range(LAYERS)
    ]
    half = half_weights(packed[0], core)
    after, before = ahead(half, 1), ahead(half, 3)
    far = far_weights(after, before)
    theirs = [other_core(after), other_core(before)]
    far, *theirs, in0, out0 = tie(far, *theirs, expert_in[0, 0], expert_out[0, 0])
    weights0 = [packed[0], after, far, before, theirs[0], other_core(far), theirs[1]]
    next_in, last_out = ahead(in0, 1), ahead(out0, 3)
    next_out, last_in = ahead(out0, 1), ahead(in0, 3)
    order = (me + jnp.arange(parts)) % parts
    hidden_bias = [jnp.take(ebias[:, layer], order, axis=0) for layer in range(LAYERS)]
    targets = [
        jnp.pad(slot_targets(routes[layer], experts, stride), fill, constant_values=-1)
        for layer in range(LAYERS)
    ]
    turned = [a.T for a in targets]
    named = [jnp.pad(routes[layer], fill) for layer in range(LAYERS)]
    bias_out = [expert_out_bias[layer].astype(F32) for layer in range(LAYERS)]
    x0 = jnp.pad(tokens, fill).astype(F32)
    cot = jnp.pad(cotangent, fill).astype(F32)

    kept_shapes = [shaped((held, width), BF16)] * 4 + [
        shaped((held, 128), F32),
        shaped((held, experts), F32),
        shaped((held, 2), F32),
    ]
    full_rows = shaped((held, width), F32)

    full_shape = shaped((4, width, width), BF16)

    def mixer_forward(first, args, outs):
        return pl.pallas_call(
            functools.partial(mixer_forward_body, first, count, scale, experts),
            out_shape=outs + [full_shape],
            in_specs=[pl.BlockSpec(memory_space=pltpu.SMEM)]
            + [pl.BlockSpec(memory_space=pltpu.VMEM)] * (len(args) - 1),
            compiler_params=pltpu.CompilerParams(vmem_limit_bytes=VMEM_LIMIT),
            cost_estimate=pl.CostEstimate(
                flops=2_000_000_000, bytes_accessed=20_000_000, transcendentals=0
            ),
        )(*args)

    middle0, send, *kept0 = mixer_forward(
        True,
        (here, *weights0, x0, lane_rows[0], routers[0], rbias[0], named[0], turned[0]),
        [full_rows, shaped((rows, width), BF16)] + kept_shapes,
    )
    full0 = kept0.pop()
    rows0 = swap(send, stride)
    bias = hidden_bias[0]
    total, slope_own = expert_pieces(
        rows0, None, [(in0, out0)], bias[0:1], None, bias_out[0], False
    )
    total, next_in, next_out, last_in, last_out, dense_next = tie(
        total, next_in, next_out, last_in, last_out, packed[1]
    )
    half = half_weights(dense_next, core)
    after, before = ahead(half, 1), ahead(half, 3)
    far_in, far_out = ahead(next_in, 1), ahead(last_out, 3)
    total, slope_near = expert_pieces(
        rows0,
        None,
        [(next_in, next_out), (last_in, last_out)],
        bias[1::2],
        None,
        total,
        False,
    )
    total, after, before = tie(total, after, before)
    far = far_weights(after, before)
    theirs = [other_core(after), other_core(before)]
    result, slope_far = expert_pieces(
        rows0, None, [(far_in, far_out)], bias[2:3], None, total, True
    )
    wide0 = [(in0, out0), (next_in, next_out), (far_in, far_out), (last_in, last_out)]
    far, *theirs, in1, out1, _ = tie(far, *theirs, expert_in[1, 0], expert_out[1, 0], far_in)
    weights1 = [packed[1], after, far, before, theirs[0], other_core(far), theirs[1]]
    next_in, last_out = ahead(in1, 1), ahead(out1, 3)
    y0 = swap(result, stride)
    gates0 = kept0[6]
    middle1, send, *kept1 = mixer_forward(
        False,
        (here, *weights1, middle0, y0, gates0, targets[0], cot)
        + (lane_rows[1], routers[1], rbias[1], named[1], turned[1]),
        [full_rows, shaped((rows, 2 * width), BF16)] + kept_shapes + [full_rows],
    )
    full1 = kept1.pop()
    x1 = kept1.pop()
    send, next_in, last_out = tie(send, next_in, last_out)
    next_out, last_in = ahead(out1, 1), ahead(in1, 3)
    far_in, far_out = ahead(next_in, 1), ahead(last_out, 3)
    both1 = swap(send, stride)
    wide1 = [(in1, out1), (next_in, next_out), (far_in, far_out), (last_in, last_out)]
    (both,) = expert_pieces(both1, both1, wide1, hidden_bias[1], None, bias_out[1], True)
    after1, before1, far1 = ring_rows(both1)
    early, _ = tie(rows0, both1)
    after0, before0, far0 = ring_rows(early)
    both = swap(both, stride)
    both, after1, before1, after0, before0 = tie(both, after1, before1, after0, before0)
    joint1 = [both1, after1, before1, *far1(after1, before1)]
    rows_pieces = [rows0, after0, before0, *far0(after0, before0)]

    half_shape = shaped((parts, 2, part, width), BF16)
    small_shape = shaped((40, width), F32)
    scratch = [pltpu.VMEM((held, width), BF16)] * 4

    def mixer_backward(last, args, outs):
        specs = [pl.BlockSpec(memory_space=pltpu.VMEM)] * len(args)
        specs[13] = pl.BlockSpec(memory_space=pltpu.SMEM)
        return pl.pallas_call(
            functools.partial(mixer_backward_body, last, count, scale, experts),
            out_shape=outs,
            in_specs=specs,
            scratch_shapes=scratch,
            compiler_params=pltpu.CompilerParams(vmem_limit_bytes=VMEM_LIMIT),
            cost_estimate=pl.CostEstimate(
                flops=4_000_000_000, bytes_accessed=20_000_000, transcendentals=0
            ),
        )(*args)

    q, k, v, m, lse, probs, gates = kept1
    g, keep1, give1, small1, activations, send = mixer_backward(
        True,
        (cot, both, x1, middle1, q, k, v, m, lse, probs, gates, named[1], targets[1])
        + (here, full1, lane_rows[1], routers[1], turned[0], gates0),
        [
            full_rows,
            half_shape,
            half_shape,
            small_shape,
            shaped((held, width), BF16),
            shaped((rows, width), BF16),
        ],
    )
    size = lax.axis_size("expert")
    same_core = [[i for i in range(size) if i % 2 == c] for c in range(2)]

    def chip_sum(keep, give, more=None):
        chip = (keep.astype(F32) + other_core(give).astype(F32)).astype(BF16)
        chip = chip.reshape(parts, 2 * part, width)
        if more is None:
            return chip
        paired = more.astype(BF16).reshape(2, -1, width)
        mine = lax.dynamic_index_in_dim(paired, core, 0, keepdims=False).astype(F32)
        theirs = lax.dynamic_index_in_dim(paired, 1 - core, 0, keepdims=False)
        mine = (mine + other_core(theirs).astype(F32)).astype(BF16)
        return jnp.concatenate(
            [chip, jnp.broadcast_to(mine[None], (parts,) + mine.shape)], axis=1
        )

    def line_sum(chip):
        spot = lambda step: lax.dynamic_index_in_dim(
            chip, (me + step) % parts, 0, keepdims=False
        )
        got = [ahead(spot(step), parts - step) for step in range(1, parts)]
        return sum([a.astype(F32) for a in got], spot(0).astype(F32)).astype(BF16)

    line1 = line_sum(chip_sum(keep1, give1))
    grads0 = swap(send, stride)
    grads0, *rows_pieces = tie(grads0, *rows_pieces)
    grads0, *joint1 = tie(grads0, *joint1)
    (back0,) = expert_pieces(
        None,
        grads0,
        [wide0[i] for i in (0, 1, 3, 2)],
        None,
        [slope_own, slope_near, slope_far],
        None,
        True,
    )
    bias_columns = expert_in_bias[:, 0].astype(F32)[:, :, None]
    back0, *joint1 = tie(back0, *joint1)
    own = expert_grads(joint1, expert_in[1, 0], bias_columns[1], expert_out[1, 0], 1)
    far_rows = ahead(grads0, 2)
    grads_pieces = [grads0, ahead(grads0, 1), ahead(grads0, 3)]
    grads_pieces += [far_rows[: rows // 2], far_rows[rows // 2 :]]
    back0 = swap(back0, stride)
    back0, line1, *own = tie(back0, line1, *own)
    back0, *grads_pieces = tie(back0, *grads_pieces)
    q, k, v, m, lse, probs, gates = kept0
    g, keep0, give0, small0 = mixer_backward(
        False,
        (g, back0, x0, middle0, q, k, v, m, lse, probs, gates, named[0], targets[0])
        + (here, full0, lane_rows[0], routers[0], y0),
        [full_rows, half_shape, half_shape, small_shape],
    )

    own = expert_grads(
        list(zip(rows_pieces, grads_pieces)),
        expert_in[0, 0],
        bias_columns[0],
        expert_out[0, 0],
        0,
        own,
    )
    in_grad, in_bias_grad, out_grad, out_bias_grad = own
    smalls = jnp.concatenate([small0, small1, jnp.zeros((-80 % size, width), F32)])
    line0 = line_sum(chip_sum(keep0, give0, smalls))
    each = 2 * part * 2 // size
    lines = jnp.concatenate(
        [
            line0[: 2 * part].reshape(size // 2, each, width),
            line1.reshape(size // 2, each, width),
            line0[2 * part :].reshape(size // 2, -1, width),
        ],
        axis=1,
    )
    got = lax.all_to_all(
        lines, "expert", split_axis=0, concat_axis=0, tiled=True, axis_index_groups=same_core
    )
    final = jnp.sum(got.astype(F32), axis=0).astype(BF16)
    got = lax.all_to_all(
        jnp.broadcast_to(final[None], (size,) + final.shape),
        "expert",
        split_axis=0,
        concat_axis=0,
        tiled=True,
    )
    extra = final.shape[0] - 2 * each

    def unpack_body(got_ref, qkv_out, out_out, small_ref):
        for source in range(size):
            place, c = source // 2, source % 2
            kind = 2 * c + place * each // part
            spot = pl.ds(place * each % part, each)
            for layer in range(LAYERS):
                lines = got_ref[source, layer * each : (layer + 1) * each, :].astype(F32)
                if kind < 3:
                    qkv_out[layer, kind, spot, :] = lines
                else:
                    out_out[layer, spot, :] = lines
            start = (c * (size // 2) + place) * extra
            small_ref[start : start + extra, :] = got_ref[source, 2 * each :, :].astype(F32)

    qkv_grad, out_weight_grad, smalls = pl.pallas_call(
        unpack_body,
        out_shape=[
            shaped((LAYERS, 3, part, width), F32),
            shaped((LAYERS, part, width), F32),
            shaped((size * extra, width), F32),
        ],
        compiler_params=pltpu.CompilerParams(vmem_limit_bytes=VMEM_LIMIT),
        cost_estimate=pl.CostEstimate(flops=0, bytes_accessed=10_000_000, transcendentals=0),
    )(got)
    small_sum = smalls[:80].reshape(LAYERS, 40, width)
    mine = lax.dynamic_slice_in_dim(small_sum, me * part, part, axis=2)
    router_grad = jnp.swapaxes(mine[:, 7 : 7 + experts], 1, 2)
    rbias_grad = lax.dynamic_slice_in_dim(
        small_sum[:, 7 + experts], me * router_bias.shape[1], router_bias.shape[1], axis=1
    )
    return (
        activations[:count],
        g[:count],
        qkv_grad,
        out_weight_grad,
        mine[:, :2],
        mine[:, 2:7],
        router_grad,
        rbias_grad,
        in_grad[:, None],
        in_bias_grad[:, None, :, 0],
        out_grad[:, None],
        out_bias_grad,
    )


def solution(mesh):
    tokens_spec = P(("expert", "fsdp"), None)
    params = (
        P(None, None, "fsdp", None),
        P(None, "fsdp", None),
        P(None, None, "fsdp"),
        P(None, None, "fsdp"),
        P(None, "fsdp", None),
        P(None, "fsdp"),
        P(None, "expert", None, "fsdp"),
        P(None, "expert", "fsdp"),
        P(None, "expert", "fsdp", None),
        P(None, "expert", None),
    )
    return jax.shard_map(
        shards,
        mesh=mesh,
        in_specs=(tokens_spec,) + params + (P(None, ("expert", "fsdp"), None), tokens_spec),
        out_specs=(tokens_spec, tokens_spec) + params,
        check_vma=False,
    )
```

```python
import functools

import jax
import jax.numpy as jnp
from jax import lax
from jax.experimental import pallas as pl
from jax.experimental.pallas import tpu as pltpu
from jax.sharding import PartitionSpec as P

HEADS = 12
LAYERS = 2
EPSILON = 1e-06
BF16 = jnp.bfloat16
F32 = jnp.float32
VMEM_LIMIT = 56 * 1024 * 1024


def dot(left, right, left_dim=1, right_dim=0):
    return lax.dot_general(
        left, right, (((left_dim,), (right_dim,)), ((), ())), preferred_element_type=F32
    )


def shaped(shape, kind):
    return jax.ShapeDtypeStruct(shape, kind)


def standardize(values):
    centred = values - jnp.mean(values, axis=-1, keepdims=True)
    inverse = lax.rsqrt(jnp.mean(centred * centred, axis=-1, keepdims=True) + EPSILON)
    return centred * inverse, inverse


def norm_backward(grad_out, scaled, inverse, gain):
    grad_scaled = grad_out * gain
    mean_grad = jnp.mean(grad_scaled, axis=-1, keepdims=True)
    mean_cross = jnp.mean(grad_scaled * scaled, axis=-1, keepdims=True)
    grad_input = inverse * (grad_scaled - mean_grad - scaled * mean_cross)
    return (
        grad_input,
        jnp.sum(grad_out * scaled, axis=0, keepdims=True),
        jnp.sum(grad_out, axis=0, keepdims=True),
    )


def gelu_both(pre):
    cdf = 0.5 + 0.5 * lax.erf(pre * (0.5**0.5))
    bell = jnp.exp2(pre * pre * (-0.5 * 1.4426950408889634))
    return pre * cdf, cdf + pre * (bell * 0.3989422804014327)


class Fetch:
    def __init__(self, sources, targets, semaphores):
        self.copies = [
            pltpu.make_async_copy(source, target, semaphores.at[i])
            for i, (source, target) in enumerate(zip(sources, targets))
        ]
        for copy in self.copies:
            copy.start()

    def wait(self, *which):
        for i in which:
            self.copies[i].wait()


def slot_targets(routes_layer, experts, stride):
    flat = routes_layer.reshape(-1)
    count = flat.shape[0]
    onehot = (flat[:, None] == jnp.arange(experts, dtype=jnp.int32)[None, :]).astype(BF16)
    below = (jnp.arange(count)[None, :] < jnp.arange(count)[:, None]).astype(BF16)
    earlier = dot(below, onehot)
    position = jnp.sum(earlier * onehot.astype(F32), axis=1).astype(jnp.int32)
    return (flat * stride + position).reshape(-1, 2)


def slot_rows(targets_row, rows, which):
    tokens = targets_row.shape[1]
    slots = lax.broadcasted_iota(jnp.int32, (rows, tokens), 0)
    return (slots == targets_row[which : which + 1, :]).astype(F32).astype(BF16)


def slot_columns(targets, rows, which):
    tokens = targets.shape[0]
    slots = lax.broadcasted_iota(jnp.int32, (tokens, rows), 1)
    return (slots == targets[:, which : which + 1]).astype(F32).astype(BF16)


def expert_hot(routes, experts, which):
    places = lax.broadcasted_iota(jnp.int32, (routes.shape[0], experts), 1)
    return (places == routes[:, which : which + 1]).astype(F32)


def pair_lanes(tokens, head):
    lanes = lax.broadcasted_iota(jnp.int32, (tokens, 128), 1)
    return (lanes // 64) == head % 2


def place_weights(here_ref, own_ref, mine, theirs, full_ref):
    _, part, _ = own_ref.shape
    parts = full_ref.shape[1] // part
    me, core = here_ref[0], here_ref[1]

    def spot(ahead):
        return pl.ds(pl.multiple_of(lax.rem(me + ahead, parts) * part, part), part)

    for kind in range(4):
        full_ref[kind, spot(0), :] = own_ref[kind]
    for ahead, (mine_ref, theirs_ref) in enumerate(zip(mine, theirs), start=1):
        for half in range(2):
            full_ref[2 * core + half, spot(ahead), :] = mine_ref[half]
            full_ref[2 * (1 - core) + half, spot(ahead), :] = theirs_ref[half]


def mixer_forward_body(first, count, scale, experts, *refs):
    here_ref, own_ref = refs[:2]
    full_ref = refs[-1]
    place_weights(here_ref, own_ref, refs[2:5], refs[5:8], full_ref)
    refs = refs[8:-1]
    if first:
        (x_ref, lane_ref, router_ref, rbias_ref, routes_ref, row_ref) = refs[:6]
        outs = refs[6:]
        x = x_ref[...]
    else:
        (
            middle_ref,
            back_ref,
            gates_prev_ref,
            targets_prev_ref,
            cot_ref,
            lane_ref,
            router_ref,
            rbias_ref,
            routes_ref,
            row_ref,
        ) = refs[:10]
        outs = refs[10:]
        x = middle_ref[...]
        back = back_ref[...]
        for j in range(2):
            picked = dot(slot_columns(targets_prev_ref[...], back.shape[0], j), back)
            x = x + gates_prev_ref[:, j : j + 1] * picked
    middle_out, send_out, q_out, k_out, v_out, m_out, lse_out, probs_out, gates_out = outs[:9]
    if not first:
        outs[9][...] = x
    tokens, width = x.shape
    lane = lane_ref[...]
    scaled, _ = standardize(x)
    normed = (scaled * lane[0:1] + lane[2:3]).astype(BF16)
    q_out[...] = (dot(normed, full_ref[0]) + lane[3:4]).astype(BF16)
    k_out[...] = dot(normed, full_ref[1]).astype(BF16)
    v_out[...] = (dot(normed, full_ref[2]) + lane[4:5]).astype(BF16)
    valid = lax.broadcasted_iota(jnp.int32, (tokens, tokens), 1) < count
    log_totals = jnp.zeros((tokens, 128), F32)
    head_lanes = lax.broadcasted_iota(jnp.int32, (tokens, 128), 1)
    for pair in range(HEADS // 2):
        cols = slice(pair * 128, pair * 128 + 128)
        q, k, v = q_out[:, cols], k_out[:, cols], v_out[:, cols]
        mixed = jnp.zeros((tokens, 128), F32)
        for head in (2 * pair, 2 * pair + 1):
            keep = pair_lanes(tokens, head)
            scores = dot(jnp.where(keep, q, jnp.zeros_like(q)), k, 1, 1) * scale
            scores = jnp.where(valid, scores, -1e30)
            top = jnp.max(scores, axis=-1, keepdims=True)
            exponent = jnp.exp(scores - top)
            total = jnp.sum(exponent, axis=-1, keepdims=True)
            weights = (exponent / total).astype(BF16)
            mixed = mixed + dot(weights, jnp.where(keep, v, jnp.zeros_like(v)))
            log_totals = jnp.where(head_lanes == head, top + jnp.log(total), log_totals)
        m_out[:, cols] = mixed.astype(BF16)
    lse_out[...] = log_totals
    middle = x + dot(m_out[...], full_ref[3]) + lane[5:6]
    middle_out[...] = middle
    scaled, _ = standardize(middle)
    normed = (scaled * lane[1:2] + lane[6:7]).astype(BF16)
    logits = dot(normed, router_ref[...], 1, 1) + rbias_ref[...]
    exponent = jnp.exp(logits - jnp.max(logits, axis=-1, keepdims=True))
    probs = exponent / jnp.sum(exponent, axis=-1, keepdims=True)
    probs_out[...] = probs
    gates = [
        jnp.sum(expert_hot(routes_ref[...], experts, j) * probs, axis=-1, keepdims=True)
        for j in range(2)
    ]
    for j in range(2):
        gates_out[:, j : j + 1] = gates[j]
    rows = send_out.shape[0]
    picks = [slot_rows(row_ref[...], rows, j) for j in range(2)]
    send_out[:, :width] = dot(picks[0] + picks[1], normed).astype(BF16)
    if not first:
        cot = cot_ref[...]
        sent = sum(dot(picks[j], (gates[j] * cot).astype(BF16)) for j in range(2))
        send_out[:, width:] = sent.astype(BF16)


def mixer_backward_body(last, count, scale, experts, *refs):
    (
        g_ref,
        back_ref,
        x_ref,
        middle_ref,
        q_ref,
        k_ref,
        v_ref,
        m_ref,
        lse_ref,
        probs_ref,
        gates_ref,
        routes_ref,
        targets_ref,
        here_ref,
        full_ref,
        lane_ref,
        router_ref,
    ) = refs[:17]
    if last:
        row_prev_ref, gates_prev_ref, g_out, keep_out, give_out, small_out = refs[17:23]
        act_out, send_out = refs[23:25]
        dq_ref, dk_ref, dv_ref, dm_ref = refs[25:]
        y_back, d_back = back_ref[:, : g_ref.shape[1]], back_ref[:, g_ref.shape[1] :]
    else:
        y_ref, g_out, keep_out, give_out, small_out = refs[17:22]
        dq_ref, dk_ref, dv_ref, dm_ref = refs[22:]
        y_back, d_back = y_ref[...], back_ref[...]
    tokens, width = g_ref.shape
    rows = y_back.shape[0]
    lane = lane_ref[...]
    g = g_ref[...]
    middle = middle_ref[...]
    picks = [slot_columns(targets_ref[...], rows, j) for j in range(2)]
    dprobs = jnp.zeros((tokens, experts), F32)
    added = middle
    for j in range(2):
        picked = dot(picks[j], y_back)
        if last:
            added = added + gates_ref[:, j : j + 1] * picked
        dgate = jnp.sum(g * picked, axis=-1, keepdims=True)
        dprobs = dprobs + expert_hot(routes_ref[...], experts, j) * dgate
    if last:
        act_out[...] = added.astype(BF16)
    probs = probs_ref[...]
    dz = (probs * (dprobs - jnp.sum(dprobs * probs, axis=-1, keepdims=True))).astype(BF16)
    scaled, inverse = standardize(middle)
    normed = (scaled * lane[1:2] + lane[6:7]).astype(BF16)
    small_out[7 : 7 + experts, :] = dot(dz, normed, 0, 0)
    rbias_grad = jnp.sum(dz.astype(F32), axis=0, keepdims=True)
    small_out[7 + experts :, :] = jnp.zeros((small_out.shape[0] - 7 - experts, width), F32)
    small_out[7 + experts : 8 + experts, :experts] = rbias_grad
    dn = dot(dz, router_ref[...]) + dot(picks[0] + picks[1], d_back)
    dmiddle, gain_second, shift_second = norm_backward(dn, scaled, inverse, lane[1:2])
    dmiddle = dmiddle + g
    small_out[1:2, :] = gain_second
    small_out[6:7, :] = shift_second
    small_out[5:6, :] = jnp.sum(dmiddle, axis=0, keepdims=True)
    branch = dmiddle.astype(BF16)
    parts = keep_out.shape[0]
    part = width // parts
    core = here_ref[1]

    def store_dense(which, value):
        def store(target):
            for f in range(parts):
                target[f, which % 2] = value[f * part : (f + 1) * part, :].astype(BF16)

        pl.when(core == which // 2)(lambda: store(keep_out))
        pl.when(core != which // 2)(lambda: store(give_out))

    store_dense(3, dot(m_ref[...], branch, 0, 0))
    dm_ref[...] = dot(branch, full_ref[3], 1, 1).astype(BF16)
    valid = lax.broadcasted_iota(jnp.int32, (tokens, tokens), 1) < count
    for pair in range(HEADS // 2):
        cols = slice(pair * 128, pair * 128 + 128)
        q, k, v, dm = q_ref[:, cols], k_ref[:, cols], v_ref[:, cols], dm_ref[:, cols]
        dq = jnp.zeros((tokens, 128), F32)
        dk = jnp.zeros((tokens, 128), F32)
        dv = jnp.zeros((tokens, 128), F32)
        zero = jnp.zeros_like(q)
        for head in (2 * pair, 2 * pair + 1):
            keep = pair_lanes(tokens, head)
            q_one, k_one = jnp.where(keep, q, zero), jnp.where(keep, k, zero)
            dm_one = jnp.where(keep, dm, zero)
            scores = dot(q_one, k, 1, 1) * scale
            weights = jnp.where(
                valid, jnp.exp(scores - lse_ref[:, head : head + 1]), 0.0
            )
            dv = dv + dot(weights.astype(BF16), dm_one, 0, 0)
            dp = dot(dm_one, v, 1, 1)
            ds = weights * (dp - jnp.sum(dp * weights, axis=-1, keepdims=True))
            ds = ds.astype(BF16)
            dq = dq + dot(ds, k_one)
            dk = dk + dot(ds, q_one, 0, 0)
        dq_ref[:, cols] = (dq * scale).astype(BF16)
        dk_ref[:, cols] = (dk * scale).astype(BF16)
        dv_ref[:, cols] = dv.astype(BF16)
    small_out[3:4, :] = jnp.sum(dq_ref[...].astype(F32), axis=0, keepdims=True)
    small_out[4:5, :] = jnp.sum(dv_ref[...].astype(F32), axis=0, keepdims=True)
    scaled, inverse = standardize(x_ref[...])
    normed = (scaled * lane[0:1] + lane[2:3]).astype(BF16)
    dn = jnp.zeros((tokens, width), F32)
    for i, ref in enumerate((dq_ref, dk_ref, dv_ref)):
        store_dense(i, dot(normed, ref[...], 0, 0))
        dn = dn + dot(ref[...], full_ref[i], 1, 1)
    dx, gain_first, shift_first = norm_backward(dn, scaled, inverse, lane[0:1])
    small_out[0:1, :] = gain_first
    small_out[2:3, :] = shift_first
    dx = dx + dmiddle
    g_out[...] = dx
    if last:
        sent = sum(
            dot(
                slot_rows(row_prev_ref[...], send_out.shape[0], j),
                (gates_prev_ref[:, j : j + 1] * dx).astype(BF16),
            )
            for j in range(2)
        )
        send_out[...] = sent.astype(BF16)


CHUNK = 768
BLOCK = 256
GRAD_CHUNK = 256


def expert_pieces(rows, grads, pieces, biases, slopes, total, finish):
    forward, backward = rows is not None, grads is not None
    count = (rows if forward else grads).shape[0]
    width, part = pieces[0][0].shape
    keep = forward and not backward
    plain = [("rows" if forward else "grads", rows if forward else grads)]
    if forward:
        plain += [("biases", biases), ("total", total)]
    fetched = [a for pair in pieces for a in pair]
    slopes = slopes or []
    spots = [(j, k) for j, value in enumerate(slopes) for k in range(value.shape[0])]
    kind = BF16 if finish else F32
    shapes = []
    if forward and backward:
        shapes.append(("both", shaped((count, 2 * width), kind)))
    elif forward:
        shapes.append(("y", shaped((count, width), kind)))
        shapes.append(("kept", shaped((len(pieces), count, part), BF16)))
    else:
        shapes.append(("d", shaped((count, width), kind)))
    held = [pltpu.VMEM(a.shape, BF16) for a in fetched]
    held += [pltpu.VMEM((count, part), BF16) for _ in spots]
    source, first = ("rows", width) if forward else ("grads", 0)
    ends = [len(plain), len(fetched), len(slopes), len(shapes), len(held)]

    def body(*refs):
        refs = list(refs)
        plain_refs, far_refs, slope_refs, out_refs, held_refs = [
            [refs.pop(0) for _ in range(n)] for n in ends
        ]
        at = dict(zip([n for n, _ in plain] + [n for n, _ in shapes], plain_refs + out_refs))
        semaphores = refs.pop()
        fetch = Fetch(
            far_refs + [slope_refs[j].at[k] for j, k in spots], held_refs, semaphores
        )
        y_sum = refs.pop(0) if forward else None
        d_sum = refs.pop(0) if backward else None
        if forward:
            y_sum[...] = jnp.broadcast_to(at["total"][...], y_sum.shape)
        if backward:
            d_sum[...] = jnp.zeros_like(d_sum)
        for i in range(len(pieces)):
            in_ref, out_ref = held_refs[2 * i], held_refs[2 * i + 1]
            fetch.wait(2 * i, 2 * i + 1)
            if spots:
                slope_ref = held_refs[2 * len(pieces) + i]
                fetch.wait(2 * len(pieces) + i)
            for c in range(0, part, CHUNK):
                cols = slice(c, c + CHUNK)
                for start in range(0, count, BLOCK):
                    here = slice(start, start + BLOCK)
                    if forward:
                        pre = dot(at["rows"][here, :width], in_ref[:, cols])
                        active, slope = gelu_both(pre + at["biases"][i : i + 1, cols])
                        y_sum[here, :] += dot(active.astype(BF16), out_ref[cols, :])
                        if not backward:
                            at["kept"][i, here, cols] = slope.astype(BF16)
                    else:
                        slope = slope_ref[here, cols].astype(F32)
                    if backward:
                        grad = dot(at[source][here, first : first + width], out_ref[cols, :], 1, 1)
                        d_sum[here, :] += dot(
                            (grad * slope).astype(BF16), in_ref[:, cols], 1, 1
                        )
        if forward and backward:
            at["both"][:, :width] = y_sum[...].astype(kind)
            at["both"][:, width:] = d_sum[...].astype(kind)
        elif forward:
            at["y"][...] = y_sum[...].astype(kind)
        else:
            at["d"][...] = d_sum[...].astype(kind)

    return pl.pallas_call(
        body,
        out_shape=[s for _, s in shapes],
        in_specs=[pl.BlockSpec(memory_space=pltpu.VMEM)] * len(plain)
        + [pl.BlockSpec(memory_space=pl.ANY)] * (len(fetched) + len(slopes)),
        scratch_shapes=held
        + [pltpu.VMEM((count, width), F32)] * (forward + backward)
        + [pltpu.SemaphoreType.DMA((len(held),))],
        compiler_params=pltpu.CompilerParams(vmem_limit_bytes=VMEM_LIMIT),
        cost_estimate=pl.CostEstimate(
            flops=4 * (forward + backward) * count * width * part * len(pieces),
            bytes_accessed=20_000_000,
            transcendentals=0,
        ),
    )(*[a for _, a in plain], *fetched, *slopes)


def expert_grads(pieces, weight_in, bias_column, weight_out, layer, others=()):
    joint = not isinstance(pieces[0], tuple)
    width, part = weight_in.shape
    operands = list(pieces) if joint else [a for pair in pieces for a in pair]
    held = len(operands)
    count = sum(a.shape[0] for a in operands) // (1 if joint else 2)

    def body(*refs):
        given, refs = refs[:held], refs[held:]
        in_ref, bias_ref, out_ref = refs[:3]
        in_out, bias_out, w_out, sum_out, turned, total, *here_refs = refs[3 + len(others) :]
        fetch = Fetch(given, here_refs[:-1], here_refs[-1])
        turned[...] = in_ref[...].astype(F32).T.astype(BF16)
        for i in range(held if joint else held // 2):
            if joint:
                fetch.wait(i)
                rows_ref, grads_ref = here_refs[i].at[:, :width], here_refs[i].at[:, width:]
            else:
                fetch.wait(2 * i, 2 * i + 1)
                rows_ref, grads_ref = here_refs[2 * i], here_refs[2 * i + 1]

            def add(ref, index, value):
                ref[index] = value if i == 0 else ref[index] + value

            for c in range(0, part, GRAD_CHUNK):
                here = slice(c, c + GRAD_CHUNK)
                pre = dot(turned[here, :], rows_ref[...], 1, 1) + bias_ref[here, :]
                active, slope = gelu_both(pre)
                add(w_out, (0, here), dot(active.astype(BF16), grads_ref[...]))
                grad = (dot(out_ref[here, :], grads_ref[...], 1, 1) * slope).astype(BF16)
                add(bias_out, (0, here), jnp.sum(grad.astype(F32), axis=1, keepdims=True))
                add(total, (here, slice(None)), dot(grad, rows_ref[...]))
            add(sum_out, 0, jnp.sum(grads_ref[...].astype(F32), axis=0, keepdims=True))
        in_out[0] = total[...].T

    shapes = [(width, part), (part, 1), (part, width), (1, width)]
    fixed = lambda a: pl.BlockSpec(a.shape, lambda i: (0,) * a.ndim)
    scratch = [pltpu.VMEM(a.shape, BF16) for a in operands]
    scratch.append(pltpu.SemaphoreType.DMA((len(operands),)))
    small = [weight_in, bias_column, weight_out]
    return pl.pallas_call(
        body,
        grid=(1,),
        in_specs=[pl.BlockSpec(memory_space=pl.ANY)] * held
        + [fixed(a) for a in small]
        + [pl.BlockSpec(memory_space=pl.ANY)] * len(others),
        out_specs=[pl.BlockSpec((1,) + a, lambda i: (layer, 0, 0)) for a in shapes],
        out_shape=[shaped((LAYERS,) + a, F32) for a in shapes],
        input_output_aliases={held + len(small) + i: i for i in range(len(others))},
        scratch_shapes=[pltpu.VMEM((part, width), BF16), pltpu.VMEM((part, width), F32)] + scratch,
        compiler_params=pltpu.CompilerParams(vmem_limit_bytes=VMEM_LIMIT),
        cost_estimate=pl.CostEstimate(
            flops=8 * count * width * part, bytes_accessed=20_000_000, transcendentals=0
        ),
    )(*operands, *small, *others)


def ahead(value, steps, axis="fsdp"):
    size = lax.axis_size(axis)
    return lax.ppermute(value, axis, [((i + steps) % size, i) for i in range(size)])


def other_core(value):
    size = lax.axis_size("expert")
    return lax.ppermute(value, "expert", [(i ^ 1, i) for i in range(size)])


def tie(*values):
    return lax.optimization_barrier(values)


def ring_rows(rows):
    half = rows.shape[0] // 2
    after, before = ahead(rows, 1), ahead(rows, 3)
    return after, before, lambda a, b: (ahead(a[:half], 1), ahead(b[half:], 3))


def half_weights(packed, core):
    return lax.dynamic_slice_in_dim(packed, 2 * core, 2, axis=0)


def far_weights(after, before):
    return jnp.concatenate([ahead(after[0:1], 1), ahead(before[1:2], 3)], axis=0)


def swap(rows, stride):
    width = rows.shape[-1]
    moved = lax.all_to_all(
        rows.reshape(-1, stride, width), "expert", split_axis=0, concat_axis=0, tiled=True
    )
    return moved.reshape(-1, width)


def pack_small(norm_gain, mixer_bias, router_weight, router_bias, expert_in_bias):
    part = norm_gain.shape[-1]
    lanes = jnp.concatenate([norm_gain, mixer_bias], axis=1)
    return jnp.concatenate(
        [
            lanes.reshape(-1, part),
            jnp.swapaxes(router_weight, 1, 2).reshape(-1, part),
            jnp.pad(router_bias, ((0, 0), (0, part - router_bias.shape[1]))),
            expert_in_bias.reshape(-1, part),
        ],
        axis=0,
    )


def shards(
    tokens,
    qkv_weight,
    out_weight,
    norm_gain,
    mixer_bias,
    router_weight,
    router_bias,
    expert_in,
    expert_in_bias,
    expert_out,
    expert_out_bias,
    routes,
    cotangent,
):
    count, width = tokens.shape
    parts = lax.axis_size("fsdp")
    experts = lax.axis_size("expert") * expert_in.shape[1]
    capacity = max(2, (3 * count + experts - 1) // experts)
    stride = -(-capacity // 8) * 8
    rows = experts * stride
    held = -(-count // 16) * 16
    part = width // parts
    scale = (width // HEADS) ** (-0.5)
    fill = ((0, held - count), (0, 0))

    small_local = pack_small(
        norm_gain, mixer_bias, router_weight, router_bias, expert_in_bias
    )
    small_all = lax.all_to_all(
        jnp.broadcast_to(small_local[None], (parts,) + small_local.shape),
        "fsdp",
        split_axis=0,
        concat_axis=0,
        tiled=True,
    )
    at_router = 7 * LAYERS
    at_rbias = at_router + LAYERS * experts
    at_ebias = at_rbias + LAYERS
    lanes = jnp.swapaxes(small_all[:, :at_rbias], 0, 1).reshape(at_rbias, width)
    lane_rows = lanes[:at_router].astype(F32).reshape(LAYERS, 7, width)
    routers = lanes[at_router:].reshape(LAYERS, experts, width)
    rbias = small_all[:, at_rbias:at_ebias, : router_bias.shape[1]]
    rbias = jnp.swapaxes(rbias, 0, 1).reshape(LAYERS, 1, experts).astype(F32)
    ebias = small_all[:, at_ebias:].reshape(parts, LAYERS, -1).astype(F32)

    me, core = lax.axis_index("fsdp"), lax.axis_index("expert") % 2
    here = jnp.stack([me, core]).astype(jnp.int32)
    packed = [
        jnp.concatenate([qkv_weight[layer], out_weight[layer][None]], axis=0)
        for layer in range(LAYERS)
    ]
    half = half_weights(packed[0], core)
    after, before = ahead(half, 1), ahead(half, 3)
    far = far_weights(after, before)
    theirs = [other_core(after), other_core(before)]
    far, *theirs, in0, out0 = tie(far, *theirs, expert_in[0, 0], expert_out[0, 0])
    weights0 = [packed[0], after, far, before, theirs[0], other_core(far), theirs[1]]
    next_in, last_out = ahead(in0, 1), ahead(out0, 3)
    next_out, last_in = ahead(out0, 1), ahead(in0, 3)
    order = (me + jnp.arange(parts)) % parts
    hidden_bias = [jnp.take(ebias[:, layer], order, axis=0) for layer in range(LAYERS)]
    targets = [
        jnp.pad(slot_targets(routes[layer], experts, stride), fill, constant_values=-1)
        for layer in range(LAYERS)
    ]
    turned = [a.T for a in targets]
    named = [jnp.pad(routes[layer], fill) for layer in range(LAYERS)]
    bias_out = [expert_out_bias[layer].astype(F32) for layer in range(LAYERS)]
    x0 = jnp.pad(tokens, fill).astype(F32)
    cot = jnp.pad(cotangent, fill).astype(F32)

    kept_shapes = [shaped((held, width), BF16)] * 4 + [
        shaped((held, 128), F32),
        shaped((held, experts), F32),
        shaped((held, 2), F32),
    ]
    full_rows = shaped((held, width), F32)

    full_shape = shaped((4, width, width), BF16)

    def mixer_forward(first, args, outs):
        return pl.pallas_call(
            functools.partial(mixer_forward_body, first, count, scale, experts),
            out_shape=outs + [full_shape],
            in_specs=[pl.BlockSpec(memory_space=pltpu.SMEM)]
            + [pl.BlockSpec(memory_space=pltpu.VMEM)] * (len(args) - 1),
            compiler_params=pltpu.CompilerParams(vmem_limit_bytes=VMEM_LIMIT),
            cost_estimate=pl.CostEstimate(
                flops=2_000_000_000, bytes_accessed=20_000_000, transcendentals=0
            ),
        )(*args)

    middle0, send, *kept0 = mixer_forward(
        True,
        (here, *weights0, x0, lane_rows[0], routers[0], rbias[0], named[0], turned[0]),
        [full_rows, shaped((rows, width), BF16)] + kept_shapes,
    )
    full0 = kept0.pop()
    rows0 = swap(send, stride)
    bias = hidden_bias[0]
    total, slope_own = expert_pieces(
        rows0, None, [(in0, out0)], bias[0:1], None, bias_out[0], False
    )
    total, next_in, next_out, last_in, last_out, dense_next = tie(
        total, next_in, next_out, last_in, last_out, packed[1]
    )
    half = half_weights(dense_next, core)
    after, before = ahead(half, 1), ahead(half, 3)
    far_in, far_out = ahead(next_in, 1), ahead(last_out, 3)
    total, slope_near = expert_pieces(
        rows0,
        None,
        [(next_in, next_out), (last_in, last_out)],
        bias[1::2],
        None,
        total,
        False,
    )
    total, after, before = tie(total, after, before)
    far = far_weights(after, before)
    theirs = [other_core(after), other_core(before)]
    result, slope_far = expert_pieces(
        rows0, None, [(far_in, far_out)], bias[2:3], None, total, True
    )
    wide0 = [(in0, out0), (next_in, next_out), (far_in, far_out), (last_in, last_out)]
    far, *theirs, in1, out1, _ = tie(far, *theirs, expert_in[1, 0], expert_out[1, 0], far_in)
    weights1 = [packed[1], after, far, before, theirs[0], other_core(far), theirs[1]]
    next_in, last_out = ahead(in1, 1), ahead(out1, 3)
    y0 = swap(result, stride)
    gates0 = kept0[6]
    middle1, send, *kept1 = mixer_forward(
        False,
        (here, *weights1, middle0, y0, gates0, targets[0], cot)
        + (lane_rows[1], routers[1], rbias[1], named[1], turned[1]),
        [full_rows, shaped((rows, 2 * width), BF16)] + kept_shapes + [full_rows],
    )
    full1 = kept1.pop()
    x1 = kept1.pop()
    send, next_in, last_out = tie(send, next_in, last_out)
    next_out, last_in = ahead(out1, 1), ahead(in1, 3)
    far_in, far_out = ahead(next_in, 1), ahead(last_out, 3)
    both1 = swap(send, stride)
    wide1 = [(in1, out1), (next_in, next_out), (far_in, far_out), (last_in, last_out)]
    (both,) = expert_pieces(both1, both1, wide1, hidden_bias[1], None, bias_out[1], True)
    after1, before1, far1 = ring_rows(both1)
    early, _ = tie(rows0, both1)
    after0, before0, far0 = ring_rows(early)
    both = swap(both, stride)
    both, after1, before1 = tie(both, after1, before1)
    joint1 = [both1, after1, before1, *far1(after1, before1)]

    half_shape = shaped((parts, 2, part, width), BF16)
    small_shape = shaped((40, width), F32)
    scratch = [pltpu.VMEM((held, width), BF16)] * 4

    def mixer_backward(last, args, outs):
        specs = [pl.BlockSpec(memory_space=pltpu.VMEM)] * len(args)
        specs[13] = pl.BlockSpec(memory_space=pltpu.SMEM)
        return pl.pallas_call(
            functools.partial(mixer_backward_body, last, count, scale, experts),
            out_shape=outs,
            in_specs=specs,
            scratch_shapes=scratch,
            compiler_params=pltpu.CompilerParams(vmem_limit_bytes=VMEM_LIMIT),
            cost_estimate=pl.CostEstimate(
                flops=4_000_000_000, bytes_accessed=20_000_000, transcendentals=0
            ),
        )(*args)

    q, k, v, m, lse, probs, gates = kept1
    g, keep1, give1, small1, activations, send = mixer_backward(
        True,
        (cot, both, x1, middle1, q, k, v, m, lse, probs, gates, named[1], targets[1])
        + (here, full1, lane_rows[1], routers[1], turned[0], gates0),
        [
            full_rows,
            half_shape,
            half_shape,
            small_shape,
            shaped((held, width), BF16),
            shaped((rows, width), BF16),
        ],
    )
    size = lax.axis_size("expert")
    same_core = [[i for i in range(size) if i % 2 == c] for c in range(2)]

    def chip_sum(keep, give, more=None):
        chip = (keep.astype(F32) + other_core(give).astype(F32)).astype(BF16)
        chip = chip.reshape(parts, 2 * part, width)
        if more is None:
            return chip
        paired = more.astype(BF16).reshape(2, -1, width)
        mine = lax.dynamic_index_in_dim(paired, core, 0, keepdims=False).astype(F32)
        theirs = lax.dynamic_index_in_dim(paired, 1 - core, 0, keepdims=False)
        mine = (mine + other_core(theirs).astype(F32)).astype(BF16)
        return jnp.concatenate(
            [chip, jnp.broadcast_to(mine[None], (parts,) + mine.shape)], axis=1
        )

    def line_sum(chip):
        spot = lambda step: lax.dynamic_index_in_dim(
            chip, (me + step) % parts, 0, keepdims=False
        )
        got = [ahead(spot(step), parts - step) for step in range(1, parts)]
        return sum([a.astype(F32) for a in got], spot(0).astype(F32)).astype(BF16)

    line1 = line_sum(chip_sum(keep1, give1))
    send, after0, before0 = tie(send, after0, before0)
    rows_pieces = [rows0, after0, before0, *far0(after0, before0)]
    grads0 = swap(send, stride)
    (back0,) = expert_pieces(
        None,
        grads0,
        [wide0[i] for i in (0, 1, 3, 2)],
        None,
        [slope_own, slope_near, slope_far],
        None,
        True,
    )
    bias_columns = expert_in_bias[:, 0].astype(F32)[:, :, None]
    back0, *joint1 = tie(back0, *joint1)
    back0, *rows_pieces = tie(back0, *rows_pieces)
    own = expert_grads(joint1, expert_in[1, 0], bias_columns[1], expert_out[1, 0], 1)
    far_rows = ahead(grads0, 2)
    grads_pieces = [grads0, ahead(grads0, 1), ahead(grads0, 3)]
    grads_pieces += [far_rows[: rows // 2], far_rows[rows // 2 :]]
    back0 = swap(back0, stride)
    back0, *own = tie(back0, *own)
    q, k, v, m, lse, probs, gates = kept0
    g, keep0, give0, small0 = mixer_backward(
        False,
        (g, back0, x0, middle0, q, k, v, m, lse, probs, gates, named[0], targets[0])
        + (here, full0, lane_rows[0], routers[0], y0),
        [full_rows, half_shape, half_shape, small_shape],
    )

    keep0, give0, line1, *grads_pieces = tie(keep0, give0, line1, *grads_pieces)
    own = expert_grads(
        list(zip(rows_pieces, grads_pieces)),
        expert_in[0, 0],
        bias_columns[0],
        expert_out[0, 0],
        0,
        own,
    )
    smalls = jnp.concatenate([small0, small1, jnp.zeros((-80 % size, width), F32)])
    line0 = line_sum(chip_sum(keep0, give0, smalls))
    line0, *own = tie(line0, *own)
    in_grad, in_bias_grad, out_grad, out_bias_grad = own
    each = 2 * part * 2 // size
    lines = jnp.concatenate(
        [
            line0[: 2 * part].reshape(size // 2, each, width),
            line1.reshape(size // 2, each, width),
            line0[2 * part :].reshape(size // 2, -1, width),
        ],
        axis=1,
    )
    got = lax.all_to_all(
        lines, "expert", split_axis=0, concat_axis=0, tiled=True, axis_index_groups=same_core
    )
    final = jnp.sum(got.astype(F32), axis=0).astype(BF16)
    got = lax.all_to_all(
        jnp.broadcast_to(final[None], (size // 2,) + final.shape),
        "expert",
        split_axis=0,
        concat_axis=0,
        tiled=True,
        axis_index_groups=same_core,
    )
    swapped = other_core(got)
    extra = final.shape[0] - 2 * each

    def unpack_body(here_ref, mine_ref, theirs_ref, qkv_out, out_out, small_ref):
        def unpack(c, got_ref):
            for place in range(size // 2):
                kind = 2 * c + place * each // part
                spot = pl.ds(place * each % part, each)
                for layer in range(LAYERS):
                    lines = got_ref[place, layer * each : (layer + 1) * each, :].astype(F32)
                    if kind < 3:
                        qkv_out[layer, kind, spot, :] = lines
                    else:
                        out_out[layer, spot, :] = lines
                start = (c * (size // 2) + place) * extra
                small_ref[start : start + extra, :] = got_ref[place, 2 * each :, :].astype(F32)

        for c in range(2):
            pl.when(here_ref[1] == c)(functools.partial(unpack, c, mine_ref))
            pl.when(here_ref[1] != c)(functools.partial(unpack, c, theirs_ref))

    qkv_grad, out_weight_grad, smalls = pl.pallas_call(
        unpack_body,
        out_shape=[
            shaped((LAYERS, 3, part, width), F32),
            shaped((LAYERS, part, width), F32),
            shaped((size * extra, width), F32),
        ],
        compiler_params=pltpu.CompilerParams(vmem_limit_bytes=VMEM_LIMIT),
        in_specs=[pl.BlockSpec(memory_space=pltpu.SMEM)]
        + [pl.BlockSpec(memory_space=pltpu.VMEM)] * 2,
        cost_estimate=pl.CostEstimate(flops=0, bytes_accessed=10_000_000, transcendentals=0),
    )(here, got, swapped)
    small_sum = smalls[:80].reshape(LAYERS, 40, width)
    mine = lax.dynamic_slice_in_dim(small_sum, me * part, part, axis=2)
    router_grad = jnp.swapaxes(mine[:, 7 : 7 + experts], 1, 2)
    rbias_grad = lax.dynamic_slice_in_dim(
        small_sum[:, 7 + experts], me * router_bias.shape[1], router_bias.shape[1], axis=1
    )
    return (
        activations[:count],
        g[:count],
        qkv_grad,
        out_weight_grad,
        mine[:, :2],
        mine[:, 2:7],
        router_grad,
        rbias_grad,
        in_grad[:, None],
        in_bias_grad[:, None, :, 0],
        out_grad[:, None],
        out_bias_grad,
    )


def solution(mesh):
    tokens_spec = P(("expert", "fsdp"), None)
    params = (
        P(None, None, "fsdp", None),
        P(None, "fsdp", None),
        P(None, None, "fsdp"),
        P(None, None, "fsdp"),
        P(None, "fsdp", None),
        P(None, "fsdp"),
        P(None, "expert", None, "fsdp"),
        P(None, "expert", "fsdp"),
        P(None, "expert", "fsdp", None),
        P(None, "expert", None),
    )
    return jax.shard_map(
        shards,
        mesh=mesh,
        in_specs=(tokens_spec,) + params + (P(None, ("expert", "fsdp"), None), tokens_spec),
        out_specs=(tokens_spec, tokens_spec) + params,
        check_vma=False,
    )
```

```python
import functools

import jax
import jax.numpy as jnp
from jax import lax
from jax.experimental import pallas as pl
from jax.experimental.pallas import tpu as pltpu
from jax.sharding import PartitionSpec as P

HEADS = 12
LAYERS = 2
EPSILON = 1e-06
BF16 = jnp.bfloat16
F32 = jnp.float32
VMEM_LIMIT = 56 * 1024 * 1024


def dot(left, right, left_dim=1, right_dim=0):
    return lax.dot_general(
        left, right, (((left_dim,), (right_dim,)), ((), ())), preferred_element_type=F32
    )


def shaped(shape, kind):
    return jax.ShapeDtypeStruct(shape, kind)


def standardize(values):
    centred = values - jnp.mean(values, axis=-1, keepdims=True)
    inverse = lax.rsqrt(jnp.mean(centred * centred, axis=-1, keepdims=True) + EPSILON)
    return centred * inverse, inverse


def norm_backward(grad_out, scaled, inverse, gain):
    grad_scaled = grad_out * gain
    mean_grad = jnp.mean(grad_scaled, axis=-1, keepdims=True)
    mean_cross = jnp.mean(grad_scaled * scaled, axis=-1, keepdims=True)
    grad_input = inverse * (grad_scaled - mean_grad - scaled * mean_cross)
    return (
        grad_input,
        jnp.sum(grad_out * scaled, axis=0, keepdims=True),
        jnp.sum(grad_out, axis=0, keepdims=True),
    )


def gelu_both(pre):
    cdf = 0.5 + 0.5 * lax.erf(pre * (0.5**0.5))
    bell = jnp.exp2(pre * pre * (-0.5 * 1.4426950408889634))
    return pre * cdf, cdf + pre * (bell * 0.3989422804014327)


class Fetch:
    def __init__(self, sources, targets, semaphores):
        self.copies = [
            pltpu.make_async_copy(source, target, semaphores.at[i])
            for i, (source, target) in enumerate(zip(sources, targets))
        ]
        for copy in self.copies:
            copy.start()

    def wait(self, *which):
        for i in which:
            self.copies[i].wait()


def slot_targets(routes_layer, experts, stride):
    flat = routes_layer.reshape(-1)
    count = flat.shape[0]
    onehot = (flat[:, None] == jnp.arange(experts, dtype=jnp.int32)[None, :]).astype(BF16)
    below = (jnp.arange(count)[None, :] < jnp.arange(count)[:, None]).astype(BF16)
    earlier = dot(below, onehot)
    position = jnp.sum(earlier * onehot.astype(F32), axis=1).astype(jnp.int32)
    return (flat * stride + position).reshape(-1, 2)


def slot_rows(targets_row, rows, which):
    tokens = targets_row.shape[1]
    slots = lax.broadcasted_iota(jnp.int32, (rows, tokens), 0)
    return (slots == targets_row[which : which + 1, :]).astype(F32).astype(BF16)


def slot_columns(targets, rows, which):
    tokens = targets.shape[0]
    slots = lax.broadcasted_iota(jnp.int32, (tokens, rows), 1)
    return (slots == targets[:, which : which + 1]).astype(F32).astype(BF16)


def expert_hot(routes, experts, which):
    places = lax.broadcasted_iota(jnp.int32, (routes.shape[0], experts), 1)
    return (places == routes[:, which : which + 1]).astype(F32)


def pair_lanes(tokens, head):
    lanes = lax.broadcasted_iota(jnp.int32, (tokens, 128), 1)
    return (lanes // 64) == head % 2


def place_weights(here_ref, own_ref, mine, theirs, full_ref):
    _, part, _ = own_ref.shape
    parts = full_ref.shape[1] // part
    me, core = here_ref[0], here_ref[1]

    def spot(ahead):
        return pl.ds(pl.multiple_of(lax.rem(me + ahead, parts) * part, part), part)

    for kind in range(4):
        full_ref[kind, spot(0), :] = own_ref[kind]
    for ahead, (mine_ref, theirs_ref) in enumerate(zip(mine, theirs), start=1):
        for half in range(2):
            full_ref[2 * core + half, spot(ahead), :] = mine_ref[half]
            full_ref[2 * (1 - core) + half, spot(ahead), :] = theirs_ref[half]


def mixer_forward_body(first, count, scale, experts, *refs):
    here_ref, own_ref = refs[:2]
    full_ref = refs[-1]
    place_weights(here_ref, own_ref, refs[2:5], refs[5:8], full_ref)
    refs = refs[8:-1]
    if first:
        (x_ref, lane_ref, router_ref, rbias_ref, routes_ref, row_ref) = refs[:6]
        outs = refs[6:]
        x = x_ref[...]
    else:
        (
            middle_ref,
            back_ref,
            gates_prev_ref,
            targets_prev_ref,
            cot_ref,
            lane_ref,
            router_ref,
            rbias_ref,
            routes_ref,
            row_ref,
        ) = refs[:10]
        outs = refs[10:]
        x = middle_ref[...]
        back = back_ref[...]
        for j in range(2):
            picked = dot(slot_columns(targets_prev_ref[...], back.shape[0], j), back)
            x = x + gates_prev_ref[:, j : j + 1] * picked
    middle_out, send_out, q_out, k_out, v_out, m_out, lse_out, probs_out, gates_out = outs[:9]
    if not first:
        outs[9][...] = x
    tokens, width = x.shape
    lane = lane_ref[...]
    scaled, _ = standardize(x)
    normed = (scaled * lane[0:1] + lane[2:3]).astype(BF16)
    q_out[...] = (dot(normed, full_ref[0]) + lane[3:4]).astype(BF16)
    k_out[...] = dot(normed, full_ref[1]).astype(BF16)
    v_out[...] = (dot(normed, full_ref[2]) + lane[4:5]).astype(BF16)
    valid = lax.broadcasted_iota(jnp.int32, (tokens, tokens), 1) < count
    log_totals = jnp.zeros((tokens, 128), F32)
    head_lanes = lax.broadcasted_iota(jnp.int32, (tokens, 128), 1)
    for pair in range(HEADS // 2):
        cols = slice(pair * 128, pair * 128 + 128)
        q, k, v = q_out[:, cols], k_out[:, cols], v_out[:, cols]
        mixed = jnp.zeros((tokens, 128), F32)
        for head in (2 * pair, 2 * pair + 1):
            keep = pair_lanes(tokens, head)
            scores = dot(jnp.where(keep, q, jnp.zeros_like(q)), k, 1, 1) * scale
            scores = jnp.where(valid, scores, -1e30)
            top = jnp.max(scores, axis=-1, keepdims=True)
            exponent = jnp.exp(scores - top)
            total = jnp.sum(exponent, axis=-1, keepdims=True)
            weights = (exponent / total).astype(BF16)
            mixed = mixed + dot(weights, jnp.where(keep, v, jnp.zeros_like(v)))
            log_totals = jnp.where(head_lanes == head, top + jnp.log(total), log_totals)
        m_out[:, cols] = mixed.astype(BF16)
    lse_out[...] = log_totals
    middle = x + dot(m_out[...], full_ref[3]) + lane[5:6]
    middle_out[...] = middle
    scaled, _ = standardize(middle)
    normed = (scaled * lane[1:2] + lane[6:7]).astype(BF16)
    logits = dot(normed, router_ref[...], 1, 1) + rbias_ref[...]
    exponent = jnp.exp(logits - jnp.max(logits, axis=-1, keepdims=True))
    probs = exponent / jnp.sum(exponent, axis=-1, keepdims=True)
    probs_out[...] = probs
    gates = [
        jnp.sum(expert_hot(routes_ref[...], experts, j) * probs, axis=-1, keepdims=True)
        for j in range(2)
    ]
    for j in range(2):
        gates_out[:, j : j + 1] = gates[j]
    rows = send_out.shape[0]
    picks = [slot_rows(row_ref[...], rows, j) for j in range(2)]
    send_out[:, :width] = dot(picks[0] + picks[1], normed).astype(BF16)
    if not first:
        cot = cot_ref[...]
        sent = sum(dot(picks[j], (gates[j] * cot).astype(BF16)) for j in range(2))
        send_out[:, width:] = sent.astype(BF16)


def mixer_backward_body(last, count, scale, experts, *refs):
    (
        g_ref,
        back_ref,
        x_ref,
        middle_ref,
        q_ref,
        k_ref,
        v_ref,
        m_ref,
        lse_ref,
        probs_ref,
        gates_ref,
        routes_ref,
        targets_ref,
        here_ref,
        full_ref,
        lane_ref,
        router_ref,
    ) = refs[:17]
    if last:
        row_prev_ref, gates_prev_ref, g_out, keep_out, give_out, small_out = refs[17:23]
        act_out, send_out = refs[23:25]
        dq_ref, dk_ref, dv_ref, dm_ref = refs[25:]
        y_back, d_back = back_ref[:, : g_ref.shape[1]], back_ref[:, g_ref.shape[1] :]
    else:
        y_ref, g_out, keep_out, give_out, small_out = refs[17:22]
        dq_ref, dk_ref, dv_ref, dm_ref = refs[22:]
        y_back, d_back = y_ref[...], back_ref[...]
    tokens, width = g_ref.shape
    rows = y_back.shape[0]
    lane = lane_ref[...]
    g = g_ref[...]
    middle = middle_ref[...]
    picks = [slot_columns(targets_ref[...], rows, j) for j in range(2)]
    dprobs = jnp.zeros((tokens, experts), F32)
    added = middle
    for j in range(2):
        picked = dot(picks[j], y_back)
        if last:
            added = added + gates_ref[:, j : j + 1] * picked
        dgate = jnp.sum(g * picked, axis=-1, keepdims=True)
        dprobs = dprobs + expert_hot(routes_ref[...], experts, j) * dgate
    if last:
        act_out[...] = added.astype(BF16)
    probs = probs_ref[...]
    dz = (probs * (dprobs - jnp.sum(dprobs * probs, axis=-1, keepdims=True))).astype(BF16)
    scaled, inverse = standardize(middle)
    normed = (scaled * lane[1:2] + lane[6:7]).astype(BF16)
    small_out[7 : 7 + experts, :] = dot(dz, normed, 0, 0)
    rbias_grad = jnp.sum(dz.astype(F32), axis=0, keepdims=True)
    small_out[7 + experts :, :] = jnp.zeros((small_out.shape[0] - 7 - experts, width), F32)
    small_out[7 + experts : 8 + experts, :experts] = rbias_grad
    dn = dot(dz, router_ref[...]) + dot(picks[0] + picks[1], d_back)
    dmiddle, gain_second, shift_second = norm_backward(dn, scaled, inverse, lane[1:2])
    dmiddle = dmiddle + g
    small_out[1:2, :] = gain_second
    small_out[6:7, :] = shift_second
    small_out[5:6, :] = jnp.sum(dmiddle, axis=0, keepdims=True)
    branch = dmiddle.astype(BF16)
    parts = keep_out.shape[0]
    part = width // parts
    core = here_ref[1]

    def store_dense(which, value):
        def store(target):
            for f in range(parts):
                target[f, which % 2] = value[f * part : (f + 1) * part, :].astype(BF16)

        pl.when(core == which // 2)(lambda: store(keep_out))
        pl.when(core != which // 2)(lambda: store(give_out))

    store_dense(3, dot(m_ref[...], branch, 0, 0))
    dm_ref[...] = dot(branch, full_ref[3], 1, 1).astype(BF16)
    valid = lax.broadcasted_iota(jnp.int32, (tokens, tokens), 1) < count
    for pair in range(HEADS // 2):
        cols = slice(pair * 128, pair * 128 + 128)
        q, k, v, dm = q_ref[:, cols], k_ref[:, cols], v_ref[:, cols], dm_ref[:, cols]
        dq = jnp.zeros((tokens, 128), F32)
        dk = jnp.zeros((tokens, 128), F32)
        dv = jnp.zeros((tokens, 128), F32)
        zero = jnp.zeros_like(q)
        for head in (2 * pair, 2 * pair + 1):
            keep = pair_lanes(tokens, head)
            q_one, k_one = jnp.where(keep, q, zero), jnp.where(keep, k, zero)
            dm_one = jnp.where(keep, dm, zero)
            scores = dot(q_one, k, 1, 1) * scale
            weights = jnp.where(
                valid, jnp.exp(scores - lse_ref[:, head : head + 1]), 0.0
            )
            dv = dv + dot(weights.astype(BF16), dm_one, 0, 0)
            dp = dot(dm_one, v, 1, 1)
            ds = weights * (dp - jnp.sum(dp * weights, axis=-1, keepdims=True))
            ds = ds.astype(BF16)
            dq = dq + dot(ds, k_one)
            dk = dk + dot(ds, q_one, 0, 0)
        dq_ref[:, cols] = (dq * scale).astype(BF16)
        dk_ref[:, cols] = (dk * scale).astype(BF16)
        dv_ref[:, cols] = dv.astype(BF16)
    small_out[3:4, :] = jnp.sum(dq_ref[...].astype(F32), axis=0, keepdims=True)
    small_out[4:5, :] = jnp.sum(dv_ref[...].astype(F32), axis=0, keepdims=True)
    scaled, inverse = standardize(x_ref[...])
    normed = (scaled * lane[0:1] + lane[2:3]).astype(BF16)
    dn = jnp.zeros((tokens, width), F32)
    for i, ref in enumerate((dq_ref, dk_ref, dv_ref)):
        store_dense(i, dot(normed, ref[...], 0, 0))
        dn = dn + dot(ref[...], full_ref[i], 1, 1)
    dx, gain_first, shift_first = norm_backward(dn, scaled, inverse, lane[0:1])
    small_out[0:1, :] = gain_first
    small_out[2:3, :] = shift_first
    dx = dx + dmiddle
    g_out[...] = dx
    if last:
        sent = sum(
            dot(
                slot_rows(row_prev_ref[...], send_out.shape[0], j),
                (gates_prev_ref[:, j : j + 1] * dx).astype(BF16),
            )
            for j in range(2)
        )
        send_out[...] = sent.astype(BF16)


CHUNK = 768
BLOCK = 256
GRAD_CHUNK = 256


def expert_pieces(rows, grads, pieces, biases, slopes, total, finish):
    forward, backward = rows is not None, grads is not None
    count = (rows if forward else grads).shape[0]
    width, part = pieces[0][0].shape
    keep = forward and not backward
    plain = [("rows" if forward else "grads", rows if forward else grads)]
    if forward:
        plain += [("biases", biases), ("total", total)]
    fetched = [a for pair in pieces for a in pair]
    slopes = slopes or []
    spots = [(j, k) for j, value in enumerate(slopes) for k in range(value.shape[0])]
    kind = BF16 if finish else F32
    shapes = []
    if forward and backward:
        shapes.append(("both", shaped((count, 2 * width), kind)))
    elif forward:
        shapes.append(("y", shaped((count, width), kind)))
        shapes.append(("kept", shaped((len(pieces), count, part), BF16)))
    else:
        shapes.append(("d", shaped((count, width), kind)))
    held = [pltpu.VMEM(a.shape, BF16) for a in fetched]
    held += [pltpu.VMEM((count, part), BF16) for _ in spots]
    source, first = ("rows", width) if forward else ("grads", 0)
    ends = [len(plain), len(fetched), len(slopes), len(shapes), len(held)]

    def body(*refs):
        refs = list(refs)
        plain_refs, far_refs, slope_refs, out_refs, held_refs = [
            [refs.pop(0) for _ in range(n)] for n in ends
        ]
        at = dict(zip([n for n, _ in plain] + [n for n, _ in shapes], plain_refs + out_refs))
        semaphores = refs.pop()
        fetch = Fetch(
            far_refs + [slope_refs[j].at[k] for j, k in spots], held_refs, semaphores
        )
        y_sum = refs.pop(0) if forward else None
        d_sum = refs.pop(0) if backward else None
        if forward:
            y_sum[...] = jnp.broadcast_to(at["total"][...], y_sum.shape)
        if backward:
            d_sum[...] = jnp.zeros_like(d_sum)
        for i in range(len(pieces)):
            in_ref, out_ref = held_refs[2 * i], held_refs[2 * i + 1]
            fetch.wait(2 * i, 2 * i + 1)
            if spots:
                slope_ref = held_refs[2 * len(pieces) + i]
                fetch.wait(2 * len(pieces) + i)
            for c in range(0, part, CHUNK):
                cols = slice(c, c + CHUNK)
                for start in range(0, count, BLOCK):
                    here = slice(start, start + BLOCK)
                    if forward:
                        pre = dot(at["rows"][here, :width], in_ref[:, cols])
                        active, slope = gelu_both(pre + at["biases"][i : i + 1, cols])
                        y_sum[here, :] += dot(active.astype(BF16), out_ref[cols, :])
                        if not backward:
                            at["kept"][i, here, cols] = slope.astype(BF16)
                    else:
                        slope = slope_ref[here, cols].astype(F32)
                    if backward:
                        grad = dot(at[source][here, first : first + width], out_ref[cols, :], 1, 1)
                        d_sum[here, :] += dot(
                            (grad * slope).astype(BF16), in_ref[:, cols], 1, 1
                        )
        if forward and backward:
            at["both"][:, :width] = y_sum[...].astype(kind)
            at["both"][:, width:] = d_sum[...].astype(kind)
        elif forward:
            at["y"][...] = y_sum[...].astype(kind)
        else:
            at["d"][...] = d_sum[...].astype(kind)

    return pl.pallas_call(
        body,
        out_shape=[s for _, s in shapes],
        in_specs=[pl.BlockSpec(memory_space=pltpu.VMEM)] * len(plain)
        + [pl.BlockSpec(memory_space=pl.ANY)] * (len(fetched) + len(slopes)),
        scratch_shapes=held
        + [pltpu.VMEM((count, width), F32)] * (forward + backward)
        + [pltpu.SemaphoreType.DMA((len(held),))],
        compiler_params=pltpu.CompilerParams(vmem_limit_bytes=VMEM_LIMIT),
        cost_estimate=pl.CostEstimate(
            flops=4 * (forward + backward) * count * width * part * len(pieces),
            bytes_accessed=20_000_000,
            transcendentals=0,
        ),
    )(*[a for _, a in plain], *fetched, *slopes)


def expert_grads(pieces, weight_in, bias_column, weight_out, layer, others=()):
    joint = not isinstance(pieces[0], tuple)
    width, part = weight_in.shape
    operands = list(pieces) if joint else [a for pair in pieces for a in pair]
    held = len(operands)
    count = sum(a.shape[0] for a in operands) // (1 if joint else 2)

    def body(*refs):
        given, refs = refs[:held], refs[held:]
        in_ref, bias_ref, out_ref = refs[:3]
        in_out, bias_out, w_out, sum_out, turned, total, *here_refs = refs[3 + len(others) :]
        fetch = Fetch(given, here_refs[:-1], here_refs[-1])
        turned[...] = in_ref[...].astype(F32).T.astype(BF16)
        for i in range(held if joint else held // 2):
            if joint:
                fetch.wait(i)
                rows_ref, grads_ref = here_refs[i].at[:, :width], here_refs[i].at[:, width:]
            else:
                fetch.wait(2 * i, 2 * i + 1)
                rows_ref, grads_ref = here_refs[2 * i], here_refs[2 * i + 1]

            def add(ref, index, value):
                ref[index] = value if i == 0 else ref[index] + value

            for c in range(0, part, GRAD_CHUNK):
                here = slice(c, c + GRAD_CHUNK)
                pre = dot(turned[here, :], rows_ref[...], 1, 1) + bias_ref[here, :]
                active, slope = gelu_both(pre)
                add(w_out, (0, here), dot(active.astype(BF16), grads_ref[...]))
                grad = (dot(out_ref[here, :], grads_ref[...], 1, 1) * slope).astype(BF16)
                add(bias_out, (0, here), jnp.sum(grad.astype(F32), axis=1, keepdims=True))
                add(total, (here, slice(None)), dot(grad, rows_ref[...]))
            add(sum_out, 0, jnp.sum(grads_ref[...].astype(F32), axis=0, keepdims=True))
        in_out[0] = total[...].T

    shapes = [(width, part), (part, 1), (part, width), (1, width)]
    fixed = lambda a: pl.BlockSpec(a.shape, lambda i: (0,) * a.ndim)
    scratch = [pltpu.VMEM(a.shape, BF16) for a in operands]
    scratch.append(pltpu.SemaphoreType.DMA((len(operands),)))
    small = [weight_in, bias_column, weight_out]
    return pl.pallas_call(
        body,
        grid=(1,),
        in_specs=[pl.BlockSpec(memory_space=pl.ANY)] * held
        + [fixed(a) for a in small]
        + [pl.BlockSpec(memory_space=pl.ANY)] * len(others),
        out_specs=[pl.BlockSpec((1,) + a, lambda i: (layer, 0, 0)) for a in shapes],
        out_shape=[shaped((LAYERS,) + a, F32) for a in shapes],
        input_output_aliases={held + len(small) + i: i for i in range(len(others))},
        scratch_shapes=[pltpu.VMEM((part, width), BF16), pltpu.VMEM((part, width), F32)] + scratch,
        compiler_params=pltpu.CompilerParams(vmem_limit_bytes=VMEM_LIMIT),
        cost_estimate=pl.CostEstimate(
            flops=8 * count * width * part, bytes_accessed=20_000_000, transcendentals=0
        ),
    )(*operands, *small, *others)


def ahead(value, steps, axis="fsdp"):
    size = lax.axis_size(axis)
    return lax.ppermute(value, axis, [((i + steps) % size, i) for i in range(size)])


def other_core(value):
    size = lax.axis_size("expert")
    return lax.ppermute(value, "expert", [(i ^ 1, i) for i in range(size)])


def tie(*values):
    return lax.optimization_barrier(values)


def ring_rows(rows):
    half = rows.shape[0] // 2
    after, before = ahead(rows, 1), ahead(rows, 3)
    return after, before, lambda a, b: (ahead(a[:half], 1), ahead(b[half:], 3))


def half_weights(packed, core):
    return lax.dynamic_slice_in_dim(packed, 2 * core, 2, axis=0)


def far_weights(after, before):
    return jnp.concatenate([ahead(after[0:1], 1), ahead(before[1:2], 3)], axis=0)


def swap(rows, stride):
    width = rows.shape[-1]
    moved = lax.all_to_all(
        rows.reshape(-1, stride, width), "expert", split_axis=0, concat_axis=0, tiled=True
    )
    return moved.reshape(-1, width)


def pack_small(norm_gain, mixer_bias, router_weight, router_bias, expert_in_bias):
    part = norm_gain.shape[-1]
    lanes = jnp.concatenate([norm_gain, mixer_bias], axis=1)
    return jnp.concatenate(
        [
            lanes.reshape(-1, part),
            jnp.swapaxes(router_weight, 1, 2).reshape(-1, part),
            jnp.pad(router_bias, ((0, 0), (0, part - router_bias.shape[1]))),
            expert_in_bias.reshape(-1, part),
        ],
        axis=0,
    )


def shards(
    tokens,
    qkv_weight,
    out_weight,
    norm_gain,
    mixer_bias,
    router_weight,
    router_bias,
    expert_in,
    expert_in_bias,
    expert_out,
    expert_out_bias,
    routes,
    cotangent,
):
    count, width = tokens.shape
    parts = lax.axis_size("fsdp")
    experts = lax.axis_size("expert") * expert_in.shape[1]
    capacity = max(2, (3 * count + experts - 1) // experts)
    stride = -(-capacity // 8) * 8
    rows = experts * stride
    held = -(-count // 16) * 16
    part = width // parts
    scale = (width // HEADS) ** (-0.5)
    fill = ((0, held - count), (0, 0))

    small_local = pack_small(
        norm_gain, mixer_bias, router_weight, router_bias, expert_in_bias
    )
    small_all = lax.all_to_all(
        jnp.broadcast_to(small_local[None], (parts,) + small_local.shape),
        "fsdp",
        split_axis=0,
        concat_axis=0,
        tiled=True,
    )
    at_router = 7 * LAYERS
    at_rbias = at_router + LAYERS * experts
    at_ebias = at_rbias + LAYERS
    lanes = jnp.swapaxes(small_all[:, :at_rbias], 0, 1).reshape(at_rbias, width)
    lane_rows = lanes[:at_router].astype(F32).reshape(LAYERS, 7, width)
    routers = lanes[at_router:].reshape(LAYERS, experts, width)
    rbias = small_all[:, at_rbias:at_ebias, : router_bias.shape[1]]
    rbias = jnp.swapaxes(rbias, 0, 1).reshape(LAYERS, 1, experts).astype(F32)
    ebias = small_all[:, at_ebias:].reshape(parts, LAYERS, -1).astype(F32)

    me, core = lax.axis_index("fsdp"), lax.axis_index("expert") % 2
    here = jnp.stack([me, core]).astype(jnp.int32)
    packed = [
        jnp.concatenate([qkv_weight[layer], out_weight[layer][None]], axis=0)
        for layer in range(LAYERS)
    ]
    half = half_weights(packed[0], core)
    after, before = ahead(half, 1), ahead(half, 3)
    far = far_weights(after, before)
    theirs = [other_core(after), other_core(before)]
    *theirs, in0, out0 = tie(*theirs, expert_in[0, 0], expert_out[0, 0])
    weights0 = [packed[0], after, far, before, theirs[0], other_core(far), theirs[1]]
    next_in, last_out = ahead(in0, 1), ahead(out0, 3)
    next_out, last_in = ahead(out0, 1), ahead(in0, 3)
    order = (me + jnp.arange(parts)) % parts
    hidden_bias = [jnp.take(ebias[:, layer], order, axis=0) for layer in range(LAYERS)]
    targets = [
        jnp.pad(slot_targets(routes[layer], experts, stride), fill, constant_values=-1)
        for layer in range(LAYERS)
    ]
    turned = [a.T for a in targets]
    named = [jnp.pad(routes[layer], fill) for layer in range(LAYERS)]
    bias_out = [expert_out_bias[layer].astype(F32) for layer in range(LAYERS)]
    x0 = jnp.pad(tokens, fill).astype(F32)
    cot = jnp.pad(cotangent, fill).astype(F32)

    kept_shapes = [shaped((held, width), BF16)] * 4 + [
        shaped((held, 128), F32),
        shaped((held, experts), F32),
        shaped((held, 2), F32),
    ]
    full_rows = shaped((held, width), F32)

    full_shape = shaped((4, width, width), BF16)

    def mixer_forward(first, args, outs):
        return pl.pallas_call(
            functools.partial(mixer_forward_body, first, count, scale, experts),
            out_shape=outs + [full_shape],
            in_specs=[pl.BlockSpec(memory_space=pltpu.SMEM)]
            + [pl.BlockSpec(memory_space=pltpu.VMEM)] * (len(args) - 1),
            compiler_params=pltpu.CompilerParams(vmem_limit_bytes=VMEM_LIMIT),
            cost_estimate=pl.CostEstimate(
                flops=2_000_000_000, bytes_accessed=20_000_000, transcendentals=0
            ),
        )(*args)

    middle0, send, *kept0 = mixer_forward(
        True,
        (here, *weights0, x0, lane_rows[0], routers[0], rbias[0], named[0], turned[0]),
        [full_rows, shaped((rows, width), BF16)] + kept_shapes,
    )
    full0 = kept0.pop()
    rows0 = swap(send, stride)
    bias = hidden_bias[0]
    total, slope_own = expert_pieces(
        rows0, None, [(in0, out0)], bias[0:1], None, bias_out[0], False
    )
    total, next_in, next_out, last_in, last_out, dense_next = tie(
        total, next_in, next_out, last_in, last_out, packed[1]
    )
    half = half_weights(dense_next, core)
    after, before = ahead(half, 1), ahead(half, 3)
    far_in, far_out = ahead(next_in, 1), ahead(last_out, 3)
    total, slope_near = expert_pieces(
        rows0,
        None,
        [(next_in, next_out), (last_in, last_out)],
        bias[1::2],
        None,
        total,
        False,
    )
    total, after, before = tie(total, after, before)
    far = far_weights(after, before)
    theirs = [other_core(after), other_core(before)]
    result, slope_far = expert_pieces(
        rows0, None, [(far_in, far_out)], bias[2:3], None, total, True
    )
    wide0 = [(in0, out0), (next_in, next_out), (far_in, far_out), (last_in, last_out)]
    far, *theirs, in1, out1, _ = tie(far, *theirs, expert_in[1, 0], expert_out[1, 0], far_in)
    weights1 = [packed[1], after, far, before, theirs[0], other_core(far), theirs[1]]
    next_in, last_out = ahead(in1, 1), ahead(out1, 3)
    y0 = swap(result, stride)
    gates0 = kept0[6]
    middle1, send, *kept1 = mixer_forward(
        False,
        (here, *weights1, middle0, y0, gates0, targets[0], cot)
        + (lane_rows[1], routers[1], rbias[1], named[1], turned[1]),
        [full_rows, shaped((rows, 2 * width), BF16)] + kept_shapes + [full_rows],
    )
    full1 = kept1.pop()
    x1 = kept1.pop()
    send, next_in, last_out = tie(send, next_in, last_out)
    next_out, last_in = ahead(out1, 1), ahead(in1, 3)
    far_in, far_out = ahead(next_in, 1), ahead(last_out, 3)
    both1 = swap(send, stride)
    wide1 = [(in1, out1), (next_in, next_out), (far_in, far_out), (last_in, last_out)]
    (both,) = expert_pieces(both1, both1, wide1, hidden_bias[1], None, bias_out[1], True)
    after1, before1, far1 = ring_rows(both1)
    early, _ = tie(rows0, both1)
    after0, before0, far0 = ring_rows(early)
    both = swap(both, stride)
    both, after1, before1 = tie(both, after1, before1)
    joint1 = [both1, after1, before1, *far1(after1, before1)]

    half_shape = shaped((parts, 2, part, width), BF16)
    small_shape = shaped((40, width), F32)
    scratch = [pltpu.VMEM((held, width), BF16)] * 4

    def mixer_backward(last, args, outs):
        specs = [pl.BlockSpec(memory_space=pltpu.VMEM)] * len(args)
        specs[13] = pl.BlockSpec(memory_space=pltpu.SMEM)
        return pl.pallas_call(
            functools.partial(mixer_backward_body, last, count, scale, experts),
            out_shape=outs,
            in_specs=specs,
            scratch_shapes=scratch,
            compiler_params=pltpu.CompilerParams(vmem_limit_bytes=VMEM_LIMIT),
            cost_estimate=pl.CostEstimate(
                flops=4_000_000_000, bytes_accessed=20_000_000, transcendentals=0
            ),
        )(*args)

    q, k, v, m, lse, probs, gates = kept1
    g, keep1, give1, small1, activations, send = mixer_backward(
        True,
        (cot, both, x1, middle1, q, k, v, m, lse, probs, gates, named[1], targets[1])
        + (here, full1, lane_rows[1], routers[1], turned[0], gates0),
        [
            full_rows,
            half_shape,
            half_shape,
            small_shape,
            shaped((held, width), BF16),
            shaped((rows, width), BF16),
        ],
    )
    size = lax.axis_size("expert")
    same_core = [[i for i in range(size) if i % 2 == c] for c in range(2)]

    def chip_sum(keep, give, more=None):
        chip = (keep.astype(F32) + other_core(give).astype(F32)).astype(BF16)
        chip = chip.reshape(parts, 2 * part, width)
        if more is None:
            return chip
        paired = more.astype(BF16).reshape(2, -1, width)
        mine = lax.dynamic_index_in_dim(paired, core, 0, keepdims=False).astype(F32)
        theirs = lax.dynamic_index_in_dim(paired, 1 - core, 0, keepdims=False)
        mine = (mine + other_core(theirs).astype(F32)).astype(BF16)
        return jnp.concatenate(
            [chip, jnp.broadcast_to(mine[None], (parts,) + mine.shape)], axis=1
        )

    def line_sum(chip):
        spot = lambda step: lax.dynamic_index_in_dim(
            chip, (me + step) % parts, 0, keepdims=False
        )
        got = [ahead(spot(step), parts - step) for step in range(1, parts)]
        return sum([a.astype(F32) for a in got], spot(0).astype(F32)).astype(BF16)

    line1 = line_sum(chip_sum(keep1, give1))
    send, after0, before0 = tie(send, after0, before0)
    rows_pieces = [rows0, after0, before0, *far0(after0, before0)]
    grads0 = swap(send, stride)
    (back0,) = expert_pieces(
        None,
        grads0,
        [wide0[i] for i in (0, 1, 3, 2)],
        None,
        [slope_own, slope_near, slope_far],
        None,
        True,
    )
    bias_columns = expert_in_bias[:, 0].astype(F32)[:, :, None]
    back0, *joint1 = tie(back0, *joint1)
    own = expert_grads(joint1, expert_in[1, 0], bias_columns[1], expert_out[1, 0], 1)
    after_g, before_g, far_g = ring_rows(grads0)
    after_g, before_g, *own = tie(after_g, before_g, *own)
    grads_pieces = [grads0, after_g, before_g, *far_g(after_g, before_g)]
    back0 = swap(back0, stride)
    back0, *own = tie(back0, *own)
    q, k, v, m, lse, probs, gates = kept0
    g, keep0, give0, small0 = mixer_backward(
        False,
        (g, back0, x0, middle0, q, k, v, m, lse, probs, gates, named[0], targets[0])
        + (here, full0, lane_rows[0], routers[0], y0),
        [full_rows, half_shape, half_shape, small_shape],
    )

    keep0, give0, line1, *rows_pieces = tie(keep0, give0, line1, *rows_pieces)
    keep0, give0, *grads_pieces = tie(keep0, give0, *grads_pieces)
    own = expert_grads(
        list(zip(rows_pieces, grads_pieces)),
        expert_in[0, 0],
        bias_columns[0],
        expert_out[0, 0],
        0,
        own,
    )
    smalls = jnp.concatenate([small0, small1, jnp.zeros((-80 % size, width), F32)])
    line0 = line_sum(chip_sum(keep0, give0, smalls))
    line0, *own = tie(line0, *own)
    in_grad, in_bias_grad, out_grad, out_bias_grad = own
    each = 2 * part * 2 // size
    lines = jnp.concatenate(
        [
            line0[: 2 * part].reshape(size // 2, each, width),
            line1.reshape(size // 2, each, width),
            line0[2 * part :].reshape(size // 2, -1, width),
        ],
        axis=1,
    )
    got = lax.all_to_all(
        lines, "expert", split_axis=0, concat_axis=0, tiled=True, axis_index_groups=same_core
    )
    final = jnp.sum(got.astype(F32), axis=0).astype(BF16)
    got = lax.all_to_all(
        jnp.broadcast_to(final[None], (size // 2,) + final.shape),
        "expert",
        split_axis=0,
        concat_axis=0,
        tiled=True,
        axis_index_groups=same_core,
    )
    swapped = other_core(got)
    extra = final.shape[0] - 2 * each

    def unpack_body(here_ref, mine_ref, theirs_ref, qkv_out, out_out, small_ref):
        def unpack(c, got_ref):
            for place in range(size // 2):
                kind = 2 * c + place * each // part
                spot = pl.ds(place * each % part, each)
                for layer in range(LAYERS):
                    lines = got_ref[place, layer * each : (layer + 1) * each, :].astype(F32)
                    if kind < 3:
                        qkv_out[layer, kind, spot, :] = lines
                    else:
                        out_out[layer, spot, :] = lines
                start = (c * (size // 2) + place) * extra
                small_ref[start : start + extra, :] = got_ref[place, 2 * each :, :].astype(F32)

        for c in range(2):
            pl.when(here_ref[1] == c)(functools.partial(unpack, c, mine_ref))
            pl.when(here_ref[1] != c)(functools.partial(unpack, c, theirs_ref))

    qkv_grad, out_weight_grad, smalls = pl.pallas_call(
        unpack_body,
        out_shape=[
            shaped((LAYERS, 3, part, width), F32),
            shaped((LAYERS, part, width), F32),
            shaped((size * extra, width), F32),
        ],
        compiler_params=pltpu.CompilerParams(vmem_limit_bytes=VMEM_LIMIT),
        in_specs=[pl.BlockSpec(memory_space=pltpu.SMEM)]
        + [pl.BlockSpec(memory_space=pltpu.VMEM)] * 2,
        cost_estimate=pl.CostEstimate(flops=0, bytes_accessed=10_000_000, transcendentals=0),
    )(here, got, swapped)
    small_sum = smalls[:80].reshape(LAYERS, 40, width)
    mine = lax.dynamic_slice_in_dim(small_sum, me * part, part, axis=2)
    router_grad = jnp.swapaxes(mine[:, 7 : 7 + experts], 1, 2)
    rbias_grad = lax.dynamic_slice_in_dim(
        small_sum[:, 7 + experts], me * router_bias.shape[1], router_bias.shape[1], axis=1
    )
    return (
        activations[:count],
        g[:count],
        qkv_grad,
        out_weight_grad,
        mine[:, :2],
        mine[:, 2:7],
        router_grad,
        rbias_grad,
        in_grad[:, None],
        in_bias_grad[:, None, :, 0],
        out_grad[:, None],
        out_bias_grad,
    )


def solution(mesh):
    tokens_spec = P(("expert", "fsdp"), None)
    params = (
        P(None, None, "fsdp", None),
        P(None, "fsdp", None),
        P(None, None, "fsdp"),
        P(None, None, "fsdp"),
        P(None, "fsdp", None),
        P(None, "fsdp"),
        P(None, "expert", None, "fsdp"),
        P(None, "expert", "fsdp"),
        P(None, "expert", "fsdp", None),
        P(None, "expert", None),
    )
    return jax.shard_map(
        shards,
        mesh=mesh,
        in_specs=(tokens_spec,) + params + (P(None, ("expert", "fsdp"), None), tokens_spec),
        out_specs=(tokens_spec, tokens_spec) + params,
        check_vma=False,
    )
```

```python
import functools

import jax
import jax.numpy as jnp
from jax import lax
from jax.experimental import pallas as pl
from jax.experimental.pallas import tpu as pltpu
from jax.sharding import PartitionSpec as P

HEADS = 12
LAYERS = 2
EPSILON = 1e-06
BF16 = jnp.bfloat16
F32 = jnp.float32
VMEM_LIMIT = 56 * 1024 * 1024


def dot(left, right, left_dim=1, right_dim=0):
    return lax.dot_general(
        left, right, (((left_dim,), (right_dim,)), ((), ())), preferred_element_type=F32
    )


def shaped(shape, kind):
    return jax.ShapeDtypeStruct(shape, kind)


def standardize(values):
    centred = values - jnp.mean(values, axis=-1, keepdims=True)
    inverse = lax.rsqrt(jnp.mean(centred * centred, axis=-1, keepdims=True) + EPSILON)
    return centred * inverse, inverse


def norm_backward(grad_out, scaled, inverse, gain):
    grad_scaled = grad_out * gain
    mean_grad = jnp.mean(grad_scaled, axis=-1, keepdims=True)
    mean_cross = jnp.mean(grad_scaled * scaled, axis=-1, keepdims=True)
    grad_input = inverse * (grad_scaled - mean_grad - scaled * mean_cross)
    return (
        grad_input,
        jnp.sum(grad_out * scaled, axis=0, keepdims=True),
        jnp.sum(grad_out, axis=0, keepdims=True),
    )


def gelu_both(pre):
    cdf = 0.5 + 0.5 * lax.erf(pre * (0.5**0.5))
    bell = jnp.exp2(pre * pre * (-0.5 * 1.4426950408889634))
    return pre * cdf, cdf + pre * (bell * 0.3989422804014327)


class Fetch:
    def __init__(self, sources, targets, semaphores):
        self.copies = [
            pltpu.make_async_copy(source, target, semaphores.at[i])
            for i, (source, target) in enumerate(zip(sources, targets))
        ]
        for copy in self.copies:
            copy.start()

    def wait(self, *which):
        for i in which:
            self.copies[i].wait()


def slot_targets(routes_layer, experts, stride):
    flat = routes_layer.reshape(-1)
    count = flat.shape[0]
    onehot = (flat[:, None] == jnp.arange(experts, dtype=jnp.int32)[None, :]).astype(BF16)
    below = (jnp.arange(count)[None, :] < jnp.arange(count)[:, None]).astype(BF16)
    earlier = dot(below, onehot)
    position = jnp.sum(earlier * onehot.astype(F32), axis=1).astype(jnp.int32)
    return (flat * stride + position).reshape(-1, 2)


def slot_rows(targets_row, rows, which):
    tokens = targets_row.shape[1]
    slots = lax.broadcasted_iota(jnp.int32, (rows, tokens), 0)
    return (slots == targets_row[which : which + 1, :]).astype(F32).astype(BF16)


def slot_columns(targets, rows, which):
    tokens = targets.shape[0]
    slots = lax.broadcasted_iota(jnp.int32, (tokens, rows), 1)
    return (slots == targets[:, which : which + 1]).astype(F32).astype(BF16)


def expert_hot(routes, experts, which):
    places = lax.broadcasted_iota(jnp.int32, (routes.shape[0], experts), 1)
    return (places == routes[:, which : which + 1]).astype(F32)


def pair_lanes(tokens, head):
    lanes = lax.broadcasted_iota(jnp.int32, (tokens, 128), 1)
    return (lanes // 64) == head % 2


def place_weights(here_ref, own_ref, mine, theirs, full_ref):
    _, part, _ = own_ref.shape
    parts = full_ref.shape[1] // part
    me, core = here_ref[0], here_ref[1]

    def spot(ahead):
        return pl.ds(pl.multiple_of(lax.rem(me + ahead, parts) * part, part), part)

    for kind in range(4):
        full_ref[kind, spot(0), :] = own_ref[kind]
    for ahead, (mine_ref, theirs_ref) in enumerate(zip(mine, theirs), start=1):
        for half in range(2):
            full_ref[2 * core + half, spot(ahead), :] = mine_ref[half]
            full_ref[2 * (1 - core) + half, spot(ahead), :] = theirs_ref[half]


def mixer_forward_body(first, count, scale, experts, *refs):
    here_ref, own_ref = refs[:2]
    full_ref = refs[-1]
    place_weights(here_ref, own_ref, refs[2:5], refs[5:8], full_ref)
    refs = refs[8:-1]
    if first:
        (x_ref, lane_ref, router_ref, rbias_ref, routes_ref, row_ref) = refs[:6]
        outs = refs[6:]
        x = x_ref[...]
    else:
        (
            middle_ref,
            back_ref,
            gates_prev_ref,
            targets_prev_ref,
            cot_ref,
            lane_ref,
            router_ref,
            rbias_ref,
            routes_ref,
            row_ref,
        ) = refs[:10]
        outs = refs[10:]
        x = middle_ref[...]
        back = back_ref[...]
        for j in range(2):
            picked = dot(slot_columns(targets_prev_ref[...], back.shape[0], j), back)
            x = x + gates_prev_ref[:, j : j + 1] * picked
    middle_out, send_out, q_out, k_out, v_out, m_out, lse_out, probs_out, gates_out = outs[:9]
    if not first:
        outs[9][...] = x
    tokens, width = x.shape
    lane = lane_ref[...]
    scaled, _ = standardize(x)
    normed = (scaled * lane[0:1] + lane[2:3]).astype(BF16)
    q_out[...] = (dot(normed, full_ref[0]) + lane[3:4]).astype(BF16)
    k_out[...] = dot(normed, full_ref[1]).astype(BF16)
    v_out[...] = (dot(normed, full_ref[2]) + lane[4:5]).astype(BF16)
    valid = lax.broadcasted_iota(jnp.int32, (tokens, tokens), 1) < count
    log_totals = jnp.zeros((tokens, 128), F32)
    head_lanes = lax.broadcasted_iota(jnp.int32, (tokens, 128), 1)
    for pair in range(HEADS // 2):
        cols = slice(pair * 128, pair * 128 + 128)
        q, k, v = q_out[:, cols], k_out[:, cols], v_out[:, cols]
        mixed = jnp.zeros((tokens, 128), F32)
        for head in (2 * pair, 2 * pair + 1):
            keep = pair_lanes(tokens, head)
            scores = dot(jnp.where(keep, q, jnp.zeros_like(q)), k, 1, 1) * scale
            scores = jnp.where(valid, scores, -1e30)
            top = jnp.max(scores, axis=-1, keepdims=True)
            exponent = jnp.exp(scores - top)
            total = jnp.sum(exponent, axis=-1, keepdims=True)
            weights = (exponent / total).astype(BF16)
            mixed = mixed + dot(weights, jnp.where(keep, v, jnp.zeros_like(v)))
            log_totals = jnp.where(head_lanes == head, top + jnp.log(total), log_totals)
        m_out[:, cols] = mixed.astype(BF16)
    lse_out[...] = log_totals
    middle = x + dot(m_out[...], full_ref[3]) + lane[5:6]
    middle_out[...] = middle
    scaled, _ = standardize(middle)
    normed = (scaled * lane[1:2] + lane[6:7]).astype(BF16)
    logits = dot(normed, router_ref[...], 1, 1) + rbias_ref[...]
    exponent = jnp.exp(logits - jnp.max(logits, axis=-1, keepdims=True))
    probs = exponent / jnp.sum(exponent, axis=-1, keepdims=True)
    probs_out[...] = probs
    gates = [
        jnp.sum(expert_hot(routes_ref[...], experts, j) * probs, axis=-1, keepdims=True)
        for j in range(2)
    ]
    for j in range(2):
        gates_out[:, j : j + 1] = gates[j]
    rows = send_out.shape[0]
    picks = [slot_rows(row_ref[...], rows, j) for j in range(2)]
    send_out[:, :width] = dot(picks[0] + picks[1], normed).astype(BF16)
    if not first:
        cot = cot_ref[...]
        sent = sum(dot(picks[j], (gates[j] * cot).astype(BF16)) for j in range(2))
        send_out[:, width:] = sent.astype(BF16)


def mixer_backward_body(last, count, scale, experts, *refs):
    (
        g_ref,
        back_ref,
        x_ref,
        middle_ref,
        q_ref,
        k_ref,
        v_ref,
        m_ref,
        lse_ref,
        probs_ref,
        gates_ref,
        routes_ref,
        targets_ref,
        here_ref,
        full_ref,
        lane_ref,
        router_ref,
    ) = refs[:17]
    if last:
        row_prev_ref, gates_prev_ref, g_out, keep_out, give_out, small_out = refs[17:23]
        act_out, send_out = refs[23:25]
        dq_ref, dk_ref, dv_ref, dm_ref = refs[25:]
        y_back, d_back = back_ref[:, : g_ref.shape[1]], back_ref[:, g_ref.shape[1] :]
    else:
        y_ref, g_out, keep_out, give_out, small_out = refs[17:22]
        dq_ref, dk_ref, dv_ref, dm_ref = refs[22:]
        y_back, d_back = y_ref[...], back_ref[...]
    tokens, width = g_ref.shape
    rows = y_back.shape[0]
    lane = lane_ref[...]
    g = g_ref[...]
    middle = middle_ref[...]
    picks = [slot_columns(targets_ref[...], rows, j) for j in range(2)]
    dprobs = jnp.zeros((tokens, experts), F32)
    added = middle
    for j in range(2):
        picked = dot(picks[j], y_back)
        if last:
            added = added + gates_ref[:, j : j + 1] * picked
        dgate = jnp.sum(g * picked, axis=-1, keepdims=True)
        dprobs = dprobs + expert_hot(routes_ref[...], experts, j) * dgate
    if last:
        act_out[...] = added.astype(BF16)
    probs = probs_ref[...]
    dz = (probs * (dprobs - jnp.sum(dprobs * probs, axis=-1, keepdims=True))).astype(BF16)
    scaled, inverse = standardize(middle)
    normed = (scaled * lane[1:2] + lane[6:7]).astype(BF16)
    small_out[7 : 7 + experts, :] = dot(dz, normed, 0, 0)
    rbias_grad = jnp.sum(dz.astype(F32), axis=0, keepdims=True)
    small_out[7 + experts :, :] = jnp.zeros((small_out.shape[0] - 7 - experts, width), F32)
    small_out[7 + experts : 8 + experts, :experts] = rbias_grad
    dn = dot(dz, router_ref[...]) + dot(picks[0] + picks[1], d_back)
    dmiddle, gain_second, shift_second = norm_backward(dn, scaled, inverse, lane[1:2])
    dmiddle = dmiddle + g
    small_out[1:2, :] = gain_second
    small_out[6:7, :] = shift_second
    small_out[5:6, :] = jnp.sum(dmiddle, axis=0, keepdims=True)
    branch = dmiddle.astype(BF16)
    parts = keep_out.shape[0]
    part = width // parts
    core = here_ref[1]

    def store_dense(which, value):
        def store(target):
            for f in range(parts):
                target[f, which % 2] = value[f * part : (f + 1) * part, :].astype(BF16)

        pl.when(core == which // 2)(lambda: store(keep_out))
        pl.when(core != which // 2)(lambda: store(give_out))

    store_dense(3, dot(m_ref[...], branch, 0, 0))
    dm_ref[...] = dot(branch, full_ref[3], 1, 1).astype(BF16)
    valid = lax.broadcasted_iota(jnp.int32, (tokens, tokens), 1) < count
    for pair in range(HEADS // 2):
        cols = slice(pair * 128, pair * 128 + 128)
        q, k, v, dm = q_ref[:, cols], k_ref[:, cols], v_ref[:, cols], dm_ref[:, cols]
        dq = jnp.zeros((tokens, 128), F32)
        dk = jnp.zeros((tokens, 128), F32)
        dv = jnp.zeros((tokens, 128), F32)
        zero = jnp.zeros_like(q)
        for head in (2 * pair, 2 * pair + 1):
            keep = pair_lanes(tokens, head)
            q_one, k_one = jnp.where(keep, q, zero), jnp.where(keep, k, zero)
            dm_one = jnp.where(keep, dm, zero)
            scores = dot(q_one, k, 1, 1) * scale
            weights = jnp.where(
                valid, jnp.exp(scores - lse_ref[:, head : head + 1]), 0.0
            )
            dv = dv + dot(weights.astype(BF16), dm_one, 0, 0)
            dp = dot(dm_one, v, 1, 1)
            ds = weights * (dp - jnp.sum(dp * weights, axis=-1, keepdims=True))
            ds = ds.astype(BF16)
            dq = dq + dot(ds, k_one)
            dk = dk + dot(ds, q_one, 0, 0)
        dq_ref[:, cols] = (dq * scale).astype(BF16)
        dk_ref[:, cols] = (dk * scale).astype(BF16)
        dv_ref[:, cols] = dv.astype(BF16)
    small_out[3:4, :] = jnp.sum(dq_ref[...].astype(F32), axis=0, keepdims=True)
    small_out[4:5, :] = jnp.sum(dv_ref[...].astype(F32), axis=0, keepdims=True)
    scaled, inverse = standardize(x_ref[...])
    normed = (scaled * lane[0:1] + lane[2:3]).astype(BF16)
    dn = jnp.zeros((tokens, width), F32)
    for i, ref in enumerate((dq_ref, dk_ref, dv_ref)):
        store_dense(i, dot(normed, ref[...], 0, 0))
        dn = dn + dot(ref[...], full_ref[i], 1, 1)
    dx, gain_first, shift_first = norm_backward(dn, scaled, inverse, lane[0:1])
    small_out[0:1, :] = gain_first
    small_out[2:3, :] = shift_first
    dx = dx + dmiddle
    g_out[...] = dx
    if last:
        sent = sum(
            dot(
                slot_rows(row_prev_ref[...], send_out.shape[0], j),
                (gates_prev_ref[:, j : j + 1] * dx).astype(BF16),
            )
            for j in range(2)
        )
        send_out[...] = sent.astype(BF16)


CHUNK = 768
BLOCK = 256
GRAD_CHUNK = 256


def expert_pieces(rows, grads, pieces, biases, slopes, total, finish):
    forward, backward = rows is not None, grads is not None
    count = (rows if forward else grads).shape[0]
    width, part = pieces[0][0].shape
    keep = forward and not backward
    plain = [("rows" if forward else "grads", rows if forward else grads)]
    if forward:
        plain += [("biases", biases), ("total", total)]
    fetched = [a for pair in pieces for a in pair]
    slopes = slopes or []
    spots = [(j, k) for j, value in enumerate(slopes) for k in range(value.shape[0])]
    kind = BF16 if finish else F32
    shapes = []
    if forward and backward:
        shapes.append(("both", shaped((count, 2 * width), kind)))
    elif forward:
        shapes.append(("y", shaped((count, width), kind)))
        shapes.append(("kept", shaped((len(pieces), count, part), BF16)))
    else:
        shapes.append(("d", shaped((count, width), kind)))
    held = [pltpu.VMEM(a.shape, BF16) for a in fetched]
    held += [pltpu.VMEM((count, part), BF16) for _ in spots]
    source, first = ("rows", width) if forward else ("grads", 0)
    ends = [len(plain), len(fetched), len(slopes), len(shapes), len(held)]

    def body(*refs):
        refs = list(refs)
        plain_refs, far_refs, slope_refs, out_refs, held_refs = [
            [refs.pop(0) for _ in range(n)] for n in ends
        ]
        at = dict(zip([n for n, _ in plain] + [n for n, _ in shapes], plain_refs + out_refs))
        semaphores = refs.pop()
        fetch = Fetch(
            far_refs + [slope_refs[j].at[k] for j, k in spots], held_refs, semaphores
        )
        y_sum = refs.pop(0) if forward else None
        d_sum = refs.pop(0) if backward else None
        if forward:
            y_sum[...] = jnp.broadcast_to(at["total"][:, :width], y_sum.shape)
        if backward:
            resumed = forward and total.shape[1] > width
            d_sum[...] = at["total"][:, width:] if resumed else jnp.zeros_like(d_sum)
        for i in range(len(pieces)):
            in_ref, out_ref = held_refs[2 * i], held_refs[2 * i + 1]
            fetch.wait(2 * i, 2 * i + 1)
            if spots:
                slope_ref = held_refs[2 * len(pieces) + i]
                fetch.wait(2 * len(pieces) + i)
            for c in range(0, part, CHUNK):
                cols = slice(c, c + CHUNK)
                for start in range(0, count, BLOCK):
                    here = slice(start, start + BLOCK)
                    if forward:
                        pre = dot(at["rows"][here, :width], in_ref[:, cols])
                        active, slope = gelu_both(pre + at["biases"][i : i + 1, cols])
                        y_sum[here, :] += dot(active.astype(BF16), out_ref[cols, :])
                        if not backward:
                            at["kept"][i, here, cols] = slope.astype(BF16)
                    else:
                        slope = slope_ref[here, cols].astype(F32)
                    if backward:
                        grad = dot(at[source][here, first : first + width], out_ref[cols, :], 1, 1)
                        d_sum[here, :] += dot(
                            (grad * slope).astype(BF16), in_ref[:, cols], 1, 1
                        )
        if forward and backward:
            at["both"][:, :width] = y_sum[...].astype(kind)
            at["both"][:, width:] = d_sum[...].astype(kind)
        elif forward:
            at["y"][...] = y_sum[...].astype(kind)
        else:
            at["d"][...] = d_sum[...].astype(kind)

    return pl.pallas_call(
        body,
        out_shape=[s for _, s in shapes],
        in_specs=[pl.BlockSpec(memory_space=pltpu.VMEM)] * len(plain)
        + [pl.BlockSpec(memory_space=pl.ANY)] * (len(fetched) + len(slopes)),
        scratch_shapes=held
        + [pltpu.VMEM((count, width), F32)] * (forward + backward)
        + [pltpu.SemaphoreType.DMA((len(held),))],
        compiler_params=pltpu.CompilerParams(vmem_limit_bytes=VMEM_LIMIT),
        cost_estimate=pl.CostEstimate(
            flops=4 * (forward + backward) * count * width * part * len(pieces),
            bytes_accessed=20_000_000,
            transcendentals=0,
        ),
    )(*[a for _, a in plain], *fetched, *slopes)


def expert_grads(pieces, weight_in, bias_column, weight_out, layer, others=()):
    joint = not isinstance(pieces[0], tuple)
    width, part = weight_in.shape
    operands = list(pieces) if joint else [a for pair in pieces for a in pair]
    held = len(operands)
    count = sum(a.shape[0] for a in operands) // (1 if joint else 2)

    def body(*refs):
        given, refs = refs[:held], refs[held:]
        in_ref, bias_ref, out_ref = refs[:3]
        in_out, bias_out, w_out, sum_out, turned, total, *here_refs = refs[3 + len(others) :]
        fetch = Fetch(given, here_refs[:-1], here_refs[-1])
        turned[...] = in_ref[...].astype(F32).T.astype(BF16)
        for i in range(held if joint else held // 2):
            if joint:
                fetch.wait(i)
                rows_ref, grads_ref = here_refs[i].at[:, :width], here_refs[i].at[:, width:]
            else:
                fetch.wait(2 * i, 2 * i + 1)
                rows_ref, grads_ref = here_refs[2 * i], here_refs[2 * i + 1]

            def add(ref, index, value):
                ref[index] = value if i == 0 else ref[index] + value

            for c in range(0, part, GRAD_CHUNK):
                here = slice(c, c + GRAD_CHUNK)
                pre = dot(turned[here, :], rows_ref[...], 1, 1) + bias_ref[here, :]
                active, slope = gelu_both(pre)
                add(w_out, (0, here), dot(active.astype(BF16), grads_ref[...]))
                grad = (dot(out_ref[here, :], grads_ref[...], 1, 1) * slope).astype(BF16)
                add(bias_out, (0, here), jnp.sum(grad.astype(F32), axis=1, keepdims=True))
                add(total, (here, slice(None)), dot(grad, rows_ref[...]))
            add(sum_out, 0, jnp.sum(grads_ref[...].astype(F32), axis=0, keepdims=True))
        in_out[0] = total[...].T

    shapes = [(width, part), (part, 1), (part, width), (1, width)]
    fixed = lambda a: pl.BlockSpec(a.shape, lambda i: (0,) * a.ndim)
    scratch = [pltpu.VMEM(a.shape, BF16) for a in operands]
    scratch.append(pltpu.SemaphoreType.DMA((len(operands),)))
    small = [weight_in, bias_column, weight_out]
    return pl.pallas_call(
        body,
        grid=(1,),
        in_specs=[pl.BlockSpec(memory_space=pl.ANY)] * held
        + [fixed(a) for a in small]
        + [pl.BlockSpec(memory_space=pl.ANY)] * len(others),
        out_specs=[pl.BlockSpec((1,) + a, lambda i: (layer, 0, 0)) for a in shapes],
        out_shape=[shaped((LAYERS,) + a, F32) for a in shapes],
        input_output_aliases={held + len(small) + i: i for i in range(len(others))},
        scratch_shapes=[pltpu.VMEM((part, width), BF16), pltpu.VMEM((part, width), F32)] + scratch,
        compiler_params=pltpu.CompilerParams(vmem_limit_bytes=VMEM_LIMIT),
        cost_estimate=pl.CostEstimate(
            flops=8 * count * width * part, bytes_accessed=20_000_000, transcendentals=0
        ),
    )(*operands, *small, *others)


def ahead(value, steps, axis="fsdp"):
    size = lax.axis_size(axis)
    return lax.ppermute(value, axis, [((i + steps) % size, i) for i in range(size)])


def other_core(value):
    size = lax.axis_size("expert")
    return lax.ppermute(value, "expert", [(i ^ 1, i) for i in range(size)])


def tie(*values):
    return lax.optimization_barrier(values)


def ring_rows(rows):
    half = rows.shape[0] // 2
    after, before = ahead(rows, 1), ahead(rows, 3)
    return after, before, lambda a, b: (ahead(a[:half], 1), ahead(b[half:], 3))


def half_weights(packed, core):
    return lax.dynamic_slice_in_dim(packed, 2 * core, 2, axis=0)


def far_weights(after, before):
    return jnp.concatenate([ahead(after[0:1], 1), ahead(before[1:2], 3)], axis=0)


def swap(rows, stride):
    width = rows.shape[-1]
    moved = lax.all_to_all(
        rows.reshape(-1, stride, width), "expert", split_axis=0, concat_axis=0, tiled=True
    )
    return moved.reshape(-1, width)


def pack_small(norm_gain, mixer_bias, router_weight, router_bias, expert_in_bias):
    part = norm_gain.shape[-1]
    lanes = jnp.concatenate([norm_gain, mixer_bias], axis=1)
    return jnp.concatenate(
        [
            lanes.reshape(-1, part),
            jnp.swapaxes(router_weight, 1, 2).reshape(-1, part),
            jnp.pad(router_bias, ((0, 0), (0, part - router_bias.shape[1]))),
            expert_in_bias.reshape(-1, part),
        ],
        axis=0,
    )


def shards(
    tokens,
    qkv_weight,
    out_weight,
    norm_gain,
    mixer_bias,
    router_weight,
    router_bias,
    expert_in,
    expert_in_bias,
    expert_out,
    expert_out_bias,
    routes,
    cotangent,
):
    count, width = tokens.shape
    parts = lax.axis_size("fsdp")
    experts = lax.axis_size("expert") * expert_in.shape[1]
    capacity = max(2, (3 * count + experts - 1) // experts)
    stride = -(-capacity // 8) * 8
    rows = experts * stride
    held = -(-count // 16) * 16
    part = width // parts
    scale = (width // HEADS) ** (-0.5)
    fill = ((0, held - count), (0, 0))

    small_local = pack_small(
        norm_gain, mixer_bias, router_weight, router_bias, expert_in_bias
    )
    small_all = lax.all_to_all(
        jnp.broadcast_to(small_local[None], (parts,) + small_local.shape),
        "fsdp",
        split_axis=0,
        concat_axis=0,
        tiled=True,
    )
    at_router = 7 * LAYERS
    at_rbias = at_router + LAYERS * experts
    at_ebias = at_rbias + LAYERS
    lanes = jnp.swapaxes(small_all[:, :at_rbias], 0, 1).reshape(at_rbias, width)
    lane_rows = lanes[:at_router].astype(F32).reshape(LAYERS, 7, width)
    routers = lanes[at_router:].reshape(LAYERS, experts, width)
    rbias = small_all[:, at_rbias:at_ebias, : router_bias.shape[1]]
    rbias = jnp.swapaxes(rbias, 0, 1).reshape(LAYERS, 1, experts).astype(F32)
    ebias = small_all[:, at_ebias:].reshape(parts, LAYERS, -1).astype(F32)

    me, core = lax.axis_index("fsdp"), lax.axis_index("expert") % 2
    here = jnp.stack([me, core]).astype(jnp.int32)
    packed = [
        jnp.concatenate([qkv_weight[layer], out_weight[layer][None]], axis=0)
        for layer in range(LAYERS)
    ]
    half = half_weights(packed[0], core)
    after, before = ahead(half, 1), ahead(half, 3)
    far = far_weights(after, before)
    theirs = [other_core(after), other_core(before)]
    *theirs, in0, out0 = tie(*theirs, expert_in[0, 0], expert_out[0, 0])
    weights0 = [packed[0], after, far, before, theirs[0], other_core(far), theirs[1]]
    next_in, last_out = ahead(in0, 1), ahead(out0, 3)
    next_out, last_in = ahead(out0, 1), ahead(in0, 3)
    order = (me + jnp.arange(parts)) % parts
    hidden_bias = [jnp.take(ebias[:, layer], order, axis=0) for layer in range(LAYERS)]
    targets = [
        jnp.pad(slot_targets(routes[layer], experts, stride), fill, constant_values=-1)
        for layer in range(LAYERS)
    ]
    turned = [a.T for a in targets]
    named = [jnp.pad(routes[layer], fill) for layer in range(LAYERS)]
    bias_out = [expert_out_bias[layer].astype(F32) for layer in range(LAYERS)]
    x0 = jnp.pad(tokens, fill).astype(F32)
    cot = jnp.pad(cotangent, fill).astype(F32)

    kept_shapes = [shaped((held, width), BF16)] * 4 + [
        shaped((held, 128), F32),
        shaped((held, experts), F32),
        shaped((held, 2), F32),
    ]
    full_rows = shaped((held, width), F32)

    full_shape = shaped((4, width, width), BF16)

    def mixer_forward(first, args, outs):
        return pl.pallas_call(
            functools.partial(mixer_forward_body, first, count, scale, experts),
            out_shape=outs + [full_shape],
            in_specs=[pl.BlockSpec(memory_space=pltpu.SMEM)]
            + [pl.BlockSpec(memory_space=pltpu.VMEM)] * (len(args) - 1),
            compiler_params=pltpu.CompilerParams(vmem_limit_bytes=VMEM_LIMIT),
            cost_estimate=pl.CostEstimate(
                flops=2_000_000_000, bytes_accessed=20_000_000, transcendentals=0
            ),
        )(*args)

    middle0, send, *kept0 = mixer_forward(
        True,
        (here, *weights0, x0, lane_rows[0], routers[0], rbias[0], named[0], turned[0]),
        [full_rows, shaped((rows, width), BF16)] + kept_shapes,
    )
    full0 = kept0.pop()
    rows0 = swap(send, stride)
    bias = hidden_bias[0]
    total, slope_own = expert_pieces(
        rows0, None, [(in0, out0)], bias[0:1], None, bias_out[0], False
    )
    total, next_in, next_out, last_in, last_out, dense_next = tie(
        total, next_in, next_out, last_in, last_out, packed[1]
    )
    half = half_weights(dense_next, core)
    after, before = ahead(half, 1), ahead(half, 3)
    far_in, far_out = ahead(next_in, 1), ahead(last_out, 3)
    total, slope_near = expert_pieces(
        rows0,
        None,
        [(next_in, next_out), (last_in, last_out)],
        bias[1::2],
        None,
        total,
        False,
    )
    total, after, before = tie(total, after, before)
    far = far_weights(after, before)
    theirs = [other_core(after), other_core(before)]
    result, slope_far = expert_pieces(
        rows0, None, [(far_in, far_out)], bias[2:3], None, total, True
    )
    wide0 = [(in0, out0), (next_in, next_out), (far_in, far_out), (last_in, last_out)]
    far, *theirs, in1, out1, _ = tie(far, *theirs, expert_in[1, 0], expert_out[1, 0], far_in)
    weights1 = [packed[1], after, far, before, theirs[0], other_core(far), theirs[1]]
    next_in, last_out = ahead(in1, 1), ahead(out1, 3)
    y0 = swap(result, stride)
    gates0 = kept0[6]
    middle1, send, *kept1 = mixer_forward(
        False,
        (here, *weights1, middle0, y0, gates0, targets[0], cot)
        + (lane_rows[1], routers[1], rbias[1], named[1], turned[1]),
        [full_rows, shaped((rows, 2 * width), BF16)] + kept_shapes + [full_rows],
    )
    full1 = kept1.pop()
    x1 = kept1.pop()
    send, next_in, last_out = tie(send, next_in, last_out)
    next_out, last_in = ahead(out1, 1), ahead(in1, 3)
    far_in, far_out = ahead(next_in, 1), ahead(last_out, 3)
    both1 = swap(send, stride)
    wide1 = [(in1, out1), (next_in, next_out), (far_in, far_out), (last_in, last_out)]
    bias = hidden_bias[1]
    (sums,) = expert_pieces(
        both1,
        both1,
        [wide1[i] for i in (0, 1, 3)],
        jnp.concatenate([bias[:2], bias[3:]]),
        None,
        bias_out[1],
        False,
    )
    (both,) = expert_pieces(both1, both1, [wide1[2]], bias[2:3], None, sums, True)
    after1, before1, far1 = ring_rows(both1)
    early, _ = tie(rows0, both1)
    after0, before0, far0 = ring_rows(early)
    both = swap(both, stride)
    both, after1, before1 = tie(both, after1, before1)
    joint1 = [both1, after1, before1, *far1(after1, before1)]

    half_shape = shaped((parts, 2, part, width), BF16)
    small_shape = shaped((40, width), F32)
    scratch = [pltpu.VMEM((held, width), BF16)] * 4

    def mixer_backward(last, args, outs):
        specs = [pl.BlockSpec(memory_space=pltpu.VMEM)] * len(args)
        specs[13] = pl.BlockSpec(memory_space=pltpu.SMEM)
        return pl.pallas_call(
            functools.partial(mixer_backward_body, last, count, scale, experts),
            out_shape=outs,
            in_specs=specs,
            scratch_shapes=scratch,
            compiler_params=pltpu.CompilerParams(vmem_limit_bytes=VMEM_LIMIT),
            cost_estimate=pl.CostEstimate(
                flops=4_000_000_000, bytes_accessed=20_000_000, transcendentals=0
            ),
        )(*args)

    q, k, v, m, lse, probs, gates = kept1
    g, keep1, give1, small1, activations, send = mixer_backward(
        True,
        (cot, both, x1, middle1, q, k, v, m, lse, probs, gates, named[1], targets[1])
        + (here, full1, lane_rows[1], routers[1], turned[0], gates0),
        [
            full_rows,
            half_shape,
            half_shape,
            small_shape,
            shaped((held, width), BF16),
            shaped((rows, width), BF16),
        ],
    )
    size = lax.axis_size("expert")
    same_core = [[i for i in range(size) if i % 2 == c] for c in range(2)]

    def chip_sum(keep, give, more=None):
        chip = (keep.astype(F32) + other_core(give).astype(F32)).astype(BF16)
        chip = chip.reshape(parts, 2 * part, width)
        if more is None:
            return chip
        paired = more.astype(BF16).reshape(2, -1, width)
        mine = lax.dynamic_index_in_dim(paired, core, 0, keepdims=False).astype(F32)
        theirs = lax.dynamic_index_in_dim(paired, 1 - core, 0, keepdims=False)
        mine = (mine + other_core(theirs).astype(F32)).astype(BF16)
        return jnp.concatenate(
            [chip, jnp.broadcast_to(mine[None], (parts,) + mine.shape)], axis=1
        )

    def line_sum(chip):
        spot = lambda step: lax.dynamic_index_in_dim(
            chip, (me + step) % parts, 0, keepdims=False
        )
        got = [ahead(spot(step), parts - step) for step in range(1, parts)]
        return sum([a.astype(F32) for a in got], spot(0).astype(F32)).astype(BF16)

    line1 = line_sum(chip_sum(keep1, give1))
    send, after0, before0 = tie(send, after0, before0)
    rows_pieces = [rows0, after0, before0, *far0(after0, before0)]
    grads0 = swap(send, stride)
    (back0,) = expert_pieces(
        None,
        grads0,
        [wide0[i] for i in (0, 1, 3, 2)],
        None,
        [slope_own, slope_near, slope_far],
        None,
        True,
    )
    bias_columns = expert_in_bias[:, 0].astype(F32)[:, :, None]
    back0, *joint1 = tie(back0, *joint1)
    own = expert_grads(joint1, expert_in[1, 0], bias_columns[1], expert_out[1, 0], 1)
    after_g, before_g, far_g = ring_rows(grads0)
    after_g, before_g, *own = tie(after_g, before_g, *own)
    grads_pieces = [grads0, after_g, before_g, *far_g(after_g, before_g)]
    back0 = swap(back0, stride)
    back0, *own = tie(back0, *own)
    q, k, v, m, lse, probs, gates = kept0
    g, keep0, give0, small0 = mixer_backward(
        False,
        (g, back0, x0, middle0, q, k, v, m, lse, probs, gates, named[0], targets[0])
        + (here, full0, lane_rows[0], routers[0], y0),
        [full_rows, half_shape, half_shape, small_shape],
    )

    keep0, give0, line1, *rows_pieces = tie(keep0, give0, line1, *rows_pieces)
    keep0, give0, *grads_pieces = tie(keep0, give0, *grads_pieces)
    own = expert_grads(
        list(zip(rows_pieces, grads_pieces)),
        expert_in[0, 0],
        bias_columns[0],
        expert_out[0, 0],
        0,
        own,
    )
    smalls = jnp.concatenate([small0, small1, jnp.zeros((-80 % size, width), F32)])
    line0 = line_sum(chip_sum(keep0, give0, smalls))
    line0, *own = tie(line0, *own)
    in_grad, in_bias_grad, out_grad, out_bias_grad = own
    each = 2 * part * 2 // size
    lines = jnp.concatenate(
        [
            line0[: 2 * part].reshape(size // 2, each, width),
            line1.reshape(size // 2, each, width),
            line0[2 * part :].reshape(size // 2, -1, width),
        ],
        axis=1,
    )
    got = lax.all_to_all(
        lines, "expert", split_axis=0, concat_axis=0, tiled=True, axis_index_groups=same_core
    )
    final = jnp.sum(got.astype(F32), axis=0).astype(BF16)
    got = lax.all_to_all(
        jnp.broadcast_to(final[None], (size // 2,) + final.shape),
        "expert",
        split_axis=0,
        concat_axis=0,
        tiled=True,
        axis_index_groups=same_core,
    )
    swapped = other_core(got)
    extra = final.shape[0] - 2 * each

    def unpack_body(here_ref, mine_ref, theirs_ref, qkv_out, out_out, small_ref):
        def unpack(c, got_ref):
            for place in range(size // 2):
                kind = 2 * c + place * each // part
                spot = pl.ds(place * each % part, each)
                for layer in range(LAYERS):
                    lines = got_ref[place, layer * each : (layer + 1) * each, :].astype(F32)
                    if kind < 3:
                        qkv_out[layer, kind, spot, :] = lines
                    else:
                        out_out[layer, spot, :] = lines
                start = (c * (size // 2) + place) * extra
                small_ref[start : start + extra, :] = got_ref[place, 2 * each :, :].astype(F32)

        for c in range(2):
            pl.when(here_ref[1] == c)(functools.partial(unpack, c, mine_ref))
            pl.when(here_ref[1] != c)(functools.partial(unpack, c, theirs_ref))

    qkv_grad, out_weight_grad, smalls = pl.pallas_call(
        unpack_body,
        out_shape=[
            shaped((LAYERS, 3, part, width), F32),
            shaped((LAYERS, part, width), F32),
            shaped((size * extra, width), F32),
        ],
        compiler_params=pltpu.CompilerParams(vmem_limit_bytes=VMEM_LIMIT),
        in_specs=[pl.BlockSpec(memory_space=pltpu.SMEM)]
        + [pl.BlockSpec(memory_space=pltpu.VMEM)] * 2,
        cost_estimate=pl.CostEstimate(flops=0, bytes_accessed=10_000_000, transcendentals=0),
    )(here, got, swapped)
    small_sum = smalls[:80].reshape(LAYERS, 40, width)
    mine = lax.dynamic_slice_in_dim(small_sum, me * part, part, axis=2)
    router_grad = jnp.swapaxes(mine[:, 7 : 7 + experts], 1, 2)
    rbias_grad = lax.dynamic_slice_in_dim(
        small_sum[:, 7 + experts], me * router_bias.shape[1], router_bias.shape[1], axis=1
    )
    return (
        activations[:count],
        g[:count],
        qkv_grad,
        out_weight_grad,
        mine[:, :2],
        mine[:, 2:7],
        router_grad,
        rbias_grad,
        in_grad[:, None],
        in_bias_grad[:, None, :, 0],
        out_grad[:, None],
        out_bias_grad,
    )


def solution(mesh):
    tokens_spec = P(("expert", "fsdp"), None)
    params = (
        P(None, None, "fsdp", None),
        P(None, "fsdp", None),
        P(None, None, "fsdp"),
        P(None, None, "fsdp"),
        P(None, "fsdp", None),
        P(None, "fsdp"),
        P(None, "expert", None, "fsdp"),
        P(None, "expert", "fsdp"),
        P(None, "expert", "fsdp", None),
        P(None, "expert", None),
    )
    return jax.shard_map(
        shards,
        mesh=mesh,
        in_specs=(tokens_spec,) + params + (P(None, ("expert", "fsdp"), None), tokens_spec),
        out_specs=(tokens_spec, tokens_spec) + params,
        check_vma=False,
    )
```
